512 devices in a mesh: dp: 128 (over y, x_lo, z), expert: 4 (over x_hi, core).
Axes of the slice: x: 4 (x_hi: 2, x_lo: 2; x = x_hi * 2 + x_lo), y: 4, z: 16, core: 2. Of those that a mesh axis runs over, the one named last changes fastest.
Arguments:
- tokens: bfloat16 [384, 3072], P('dp', 'expert'), may hold values from -6 to 6
- out_grad: bfloat16 [384, 3072], P('dp', 'expert'), may hold values from -6 to 6
- expert_ids: int32 [384, 2], P('dp'), may hold values from 0 to 3, all different within a row; in each aligned block of 3 rows (0 to 2, 3 to 5, ...) at most 2 rows name the same one
- gate_weights: float32 [384, 2], P('dp'), may hold values from 0.1 to 1
- w_gate: bfloat16 [4, 3072, 16384], P('expert', None, 'dp'), may hold values from -0.109375 to 0.109375
- w_up: bfloat16 [4, 3072, 16384], P('expert', None, 'dp'), may hold values from -0.109375 to 0.109375
- w_down: bfloat16 [4, 16384, 3072], P('expert', 'dp'), may hold values from -0.046875 to 0.046875
Outputs:
- grad_tokens: bfloat16 [384, 3072], P('dp', 'expert')
- grad_gate: bfloat16 [4, 3072, 16384], P('expert', None, 'dp')
- grad_up: bfloat16 [4, 3072, 16384], P('expert', None, 'dp')
- grad_down: bfloat16 [4, 16384, 3072], P('expert', 'dp')
The draws below stay inside these ranges and needn't reach their ends.
Inputs may be any that keep to these rules, and one draw needn't show every extreme that they name: `expert_ids`: each token names two different experts. Among the 3 tokens of one index of dp (aligned blocks of rows) no expert is named more than 2 times.
All inputs are finite; a program needn't handle non-finite values.
Results may differ from the reference program's by a relative error of at most 0.0057.
Values may be sent and summed in bfloat16 or wider, within the bound.
A program may use at most 64 MiB of HBM per device.

```python
import math
import jax
import jax.numpy as jnp
import numpy as np

D = 3072
FF = 16384
TOK_DEV = 3
EXPERTS = 4
CAP = 2
ROWS = 256
TOKENS = 384


def shard_levels(rng, extent, cuts, smallest, largest):
    def one(axis_at, shards_of):
        draws = jax.random.uniform(jax.random.fold_in(jax.random.fold_in(rng, 6), axis_at), (shards_of,), jnp.float32, smallest / len(cuts), largest / len(cuts))
        return jnp.repeat(jnp.exp(draws), extent[axis_at] // shards_of).reshape((-1,) + (1,) * (len(extent) - axis_at - 1))

    gain = one(*cuts[0])
    for cut in cuts[1:]:
        gain = gain * one(*cut)
    return gain


def assign_block(key, own, number, rows, count, top, limit, slope):
    sequence = jax.random.permutation(key, count)
    packed, common = load_shares(count, rows * top, limit, slope, True), load_shares(count, rows * top, limit, slope, False)
    places = jnp.arange(count)

    def named(tallies, rotation):
        used = int((tallies > 0).sum())
        fixed = max(1, used // 4)
        moved = fixed + (places - fixed + rotation * (used - fixed)) % max(1, count - fixed)
        return jnp.zeros((count,), jnp.int32).at[sequence[jnp.where(places < fixed, places, moved)]].set(jnp.asarray(tallies, jnp.int32))

    tallies = jnp.where(number % 4 == 0, named(packed, number // 4), named(common, number - number // 4 - 1))
    mixed = jax.random.permutation(jax.random.fold_in(own, 3), count)
    giver, receiver = mixed[0:count // 2 * 2:2], mixed[1:count // 2 * 2:2]
    room = jnp.minimum(tallies[giver] - 1, limit - tallies[receiver]) // 2
    room = jnp.where((giver == sequence[0]) | (receiver == sequence[0]) | (tallies[receiver] == 0), 0, jnp.maximum(room, 0))
    moved = jax.random.randint(jax.random.fold_in(own, 4), (count // 2,), 0, 1 << 20) % (room + 1)
    tallies = tallies.at[giver].add(-moved).at[receiver].add(moved)
    labels = jnp.searchsorted(jnp.cumsum(tallies), jnp.arange(rows * top), side="right").astype(jnp.int32)
    grid = labels.reshape(top, rows).T
    grid = grid[jax.random.permutation(jax.random.fold_in(own, 1), rows)]
    rotation = jax.random.randint(jax.random.fold_in(own, 2), (rows, 1), 0, top)
    return jnp.take_along_axis(grid, (jnp.arange(top)[None, :] + rotation) % top, axis=1)


def load_shares(count, total, reach, slope, full):
    loads = [(1 << 20) // math.isqrt(standing ** slope) + 1 for standing in range(1, count + 1)]
    largest = reach if full else min(reach, max(-(-total // count), total * loads[0] // sum(loads)))
    least = 1 if total - largest >= count - 1 else 0
    counts, rest = [largest] + [least] * (count - 1), total - largest - least * (count - 1)
    while rest > 0:
        free = [i for i in range(1, count) if counts[i] < largest] or [i for i in range(1, count) if counts[i] < reach]
        mass, remaining = sum([loads[i] for i in free]), rest
        for i in free:
            addition = min(reach - counts[i], max(1, remaining * loads[i] // mass), rest)
            counts[i] = counts[i] + addition
            rest = rest - addition
    return np.array(counts)


def normal_values(rng, shape, deviation, most, cuts=(), dtype=jnp.bfloat16):
    result = jax.random.normal(rng, shape, jnp.float32) * deviation
    if len(cuts) > 0:
        result = shard_levels(rng, shape, cuts, -0.22, 0.18) * result
    return jnp.clip(result, min=-most, max=most).astype(dtype)


def setup_inputs(seed: int = 0) -> dict:
    streams_of = jax.random.split(jax.random.key(seed), 8)
    tokens = normal_values(streams_of[0], (TOKENS, D), 1.0, 6.0, ((0, 128), (1, 4)))
    out_grad = normal_values(streams_of[1], (TOKENS, D), 1.0, 6.0, ((0, 128), (1, 4)))
    expert_ids_keys = jax.random.split(jax.random.fold_in(streams_of[2], 1), TOKENS // TOK_DEV)
    expert_ids_turns = jax.random.permutation(jax.random.fold_in(streams_of[2], 3), TOKENS // TOK_DEV)
    expert_ids = jax.vmap(lambda own, number: assign_block(jax.random.fold_in(streams_of[2], 2), own, number, TOK_DEV, EXPERTS, 2, CAP, 2))(expert_ids_keys, expert_ids_turns).reshape((TOKENS, 2))
    gate_weights = jnp.clip(0.1 + 0.9 * jax.random.uniform(streams_of[3], (TOKENS, 2), jnp.float32) ** shard_levels(streams_of[3], (TOKENS, 2), ((0, 128),), -0.2, 0.2), 0.1, 1.0)
    w_gate = normal_values(streams_of[4], (EXPERTS, D, FF), D ** -0.5, 0.109375, ((0, 4), (2, 128)))
    w_up = normal_values(streams_of[5], (EXPERTS, D, FF), D ** -0.5, 0.109375, ((0, 4), (2, 128)))
    w_down = normal_values(streams_of[6], (EXPERTS, FF, D), FF ** -0.5, 0.046875, ((0, 4), (1, 128)))
    return {"tokens": tokens, "out_grad": out_grad, "expert_ids": expert_ids, "gate_weights": gate_weights, "w_gate": w_gate, "w_up": w_up, "w_down": w_down}


def reference(tokens, out_grad, expert_ids, gate_weights, w_gate, w_up, w_down):
    routed = (gate_weights[:, :, None] * out_grad[:, None, :].astype(jnp.float32)).astype(jnp.bfloat16)
    slot_rows = jnp.repeat(tokens, 2, axis=0)
    slot_grads = routed.reshape(TOKENS * 2, D)
    flat_ids = expert_ids.reshape(-1)
    grad_slots = jnp.zeros((TOKENS * 2, D), jnp.float32)
    gate_list = []
    up_list = []
    down_list = []
    for expert in range(EXPERTS):
        hits = flat_ids == expert
        places = (jnp.cumsum(hits.astype(jnp.int32)) - 1).astype(jnp.int32)
        places = jnp.where(hits, places, ROWS).astype(jnp.int32)
        rows_x = jnp.zeros((ROWS, D), jnp.bfloat16).at[places].set(slot_rows, mode="drop")
        rows_dy = jnp.zeros((ROWS, D), jnp.bfloat16).at[places].set(slot_grads, mode="drop")
        gate = jnp.dot(rows_x, w_gate[expert], preferred_element_type=jnp.float32)
        upper = jnp.dot(rows_x, w_up[expert], preferred_element_type=jnp.float32)
        sigma = jax.nn.sigmoid(gate)
        active = gate * sigma
        hidden = (active * upper).astype(jnp.bfloat16)
        down_list.append(jnp.dot(hidden.T, rows_dy, preferred_element_type=jnp.float32).astype(jnp.bfloat16))
        dhidden = jnp.dot(rows_dy, w_down[expert].T, preferred_element_type=jnp.float32)
        dgate = (dhidden * upper * (sigma + active * (1.0 - sigma))).astype(jnp.bfloat16)
        dup = (dhidden * active).astype(jnp.bfloat16)
        gate_list.append(jnp.dot(rows_x.T, dgate, preferred_element_type=jnp.float32).astype(jnp.bfloat16))
        up_list.append(jnp.dot(rows_x.T, dup, preferred_element_type=jnp.float32).astype(jnp.bfloat16))
        back = jnp.dot(dgate, w_gate[expert].T, preferred_element_type=jnp.float32)
        back = back + jnp.dot(dup, w_up[expert].T, preferred_element_type=jnp.float32)
        picked = back[jnp.minimum(places, ROWS - 1).astype(jnp.int32)]
        grad_slots = grad_slots + jnp.where(hits[:, None], picked, jnp.float32(0.0))
    grad_tokens = grad_slots.reshape(TOKENS, 2, D).sum(axis=1).astype(jnp.bfloat16)
    return grad_tokens, jnp.stack(gate_list), jnp.stack(up_list), jnp.stack(down_list)
```

```python
import jax
import jax.numpy as jnp
from jax import lax
from jax.experimental import pallas as pl
from jax.experimental.pallas import tpu as pltpu
from jax.sharding import PartitionSpec as P

MESH = pl.DeviceIdType.MESH
NX, NY, NZ = 4, 4, 16
TOK = 3
QF = 768
NQ = 4
HALF = QF // 2
GROUP = NZ * TOK
NG = 8
ROWS = NG * GROUP
HID = 128
D = NQ * QF
YW = QF + 128
BF, F32 = jnp.bfloat16, jnp.float32


def dot(a, b):
    return jnp.dot(a, b, preferred_element_type=F32)


def kernel(
    tok_ref, dy_ref, ids_ref, gw_ref, wg_hbm, wu_hbm, wd_hbm,
    gx_ref, gg_ref, gu_ref, gd_ref,
    stage, zb, tk, dy, g, wgu, wgut, wd, wdt, acts, dcat, hid, acc, sbuf, rbuf,
    sl1, rl1, sr1, rr1, sl2, rl2, sr2, rr2, sz, rz, zsum,
    w_sem, zs_sem, zr_sem, as_sem, ar_sem, ds_sem, dr_sem, es_sem, er_sem,
    ps_sem, pr_sem, qs_sem, qr_sem, fs_sem, fr_sem,
):
    dp = lax.axis_index("dp")
    ex = lax.axis_index("expert")
    z, xl, y = dp % NZ, (dp // NZ) % 2, dp // (2 * NZ)
    xh, c = ex // 2, ex % 2
    x = xh * 2 + xl

    def dev(px, py, pz, pc):
        return ((py * 2 + px % 2) * NZ + pz, (px // 2) * 2 + pc)

    def at(dx, dy_):
        return dev((x + dx) % NX, (y + dy_) % NY, z, c)

    sibling = dev(x, y, z, 1 - c)

    def zdev(d):
        return dev(x, y, (z + d) % NZ, c)

    def cell(dx, dy_):
        px, py = (x + dx) % NX, (y + dy_) % NY
        return (px // 2) * 2 + c, py * 2 + px % 2

    loads = [
        pltpu.make_async_copy(wg_hbm.at[0], wgu.at[:, pl.ds(0, HID)], w_sem.at[0]),
        pltpu.make_async_copy(wu_hbm.at[0], wgu.at[:, pl.ds(HID, HID)], w_sem.at[1]),
        pltpu.make_async_copy(wd_hbm.at[0], wd, w_sem.at[2]),
    ]
    for copy in loads:
        copy.start()

    barrier = pltpu.get_barrier_semaphore()
    peers = [zdev(d) for d in range(1, NZ)]
    peers += [at(d, 0) for d in range(1, NX)] + [at(0, d) for d in range(1, NY)] + [sibling]
    for peer in peers:
        pl.semaphore_signal(barrier, inc=1, device_id=peer, device_id_type=MESH)

    stage[...] = jnp.zeros_like(stage)
    for i, ref in enumerate((tok_ref, dy_ref)):
        v = ref[...].astype(F32)
        stage[pl.ds(6 * i, TOK), :] = v[:, :HALF]
        stage[pl.ds(6 * i + TOK, TOK), :] = v[:, HALF:]
    lane = lax.broadcasted_iota(jnp.int32, (TOK, 128), 1)
    w = jnp.zeros((TOK, 128), F32)
    for k in range(2):
        w = w + jnp.where(ids_ref[:, k : k + 1] == lane % 4, gw_ref[:, k : k + 1], 0.0)
    hi = w.astype(BF).astype(F32)
    mid = (w - hi).astype(BF).astype(F32)
    low = w - hi - mid
    w = jnp.where(lane < 4, hi, jnp.where(lane < 8, mid, jnp.where(lane < 12, low, 0.0)))
    stage[pl.ds(12, TOK), pl.ds(0, 128)] = w
    zb[z] = stage[...].astype(BF)

    pl.semaphore_wait(barrier, len(peers))

    def remote(src, dst, ssem, rsem, device):
        return pltpu.make_async_remote_copy(
            src_ref=src, dst_ref=dst, send_sem=ssem, recv_sem=rsem, device_id=device, device_id_type=MESH
        )

    sends = []

    def send(src, dst, ssem, rsem, device):
        copy = remote(src, dst, ssem, rsem, device)
        copy.start()
        sends.append(copy)

    for d in range(1, NZ):
        send(zb.at[z], zb.at[z], zs_sem.at[d], zr_sem.at[d], zdev(d))

    for copy in loads:
        copy.wait()
    for q in range(NQ):
        wgut[q] = wgu[pl.ds(q * QF, QF), :].T
        wdt[pl.ds(q * QF, QF), :] = wd[:, pl.ds(q * QF, QF)].T

    for d in range(1, NZ):
        remote(zb.at[(z - d + NZ) % NZ], zb.at[(z - d + NZ) % NZ], zs_sem.at[d], zr_sem.at[d], zdev(d)).wait_recv()

    r = lax.broadcasted_iota(jnp.int32, (5 * GROUP, NZ * 16), 0)
    s = lax.broadcasted_iota(jnp.int32, (5 * GROUP, NZ * 16), 1)
    k = s % 16
    kind = (k * 11) // 32
    pick = ((r == kind * GROUP + (s // 16) * TOK + (k - 3 * kind)) & (k < 15)).astype(F32).astype(BF)
    rows = dot(pick, zb[...].reshape(NZ * 16, HALF)).astype(BF)
    mq, mg = cell(0, 0)
    tk[mq, mg, :, pl.ds(0, HALF)] = rows[0:GROUP]
    tk[mq, mg, :, pl.ds(HALF, HALF)] = rows[GROUP : 2 * GROUP]
    dy[mq, mg, :, pl.ds(0, HALF)] = rows[2 * GROUP : 3 * GROUP]
    dy[mq, mg, :, pl.ds(HALF, HALF)] = rows[3 * GROUP : 4 * GROUP]
    dy[mq, mg, :, pl.ds(QF, 128)] = rows[4 * GROUP : 5 * GROUP, 0:128]

    arrays = ((tk, 0), (dy, 1))

    def off(h, first, second):
        return (first, second) if h == 0 else (second, first)

    def block(h, first, second):
        q_, g_ = cell(*off(h, first, second))
        return arrays[h][0].at[q_, g_]

    def to_sibling(h, first, second):
        ref = block(h, first, second)
        n = first * 4 + second
        send(ref, ref, ds_sem.at[h, n], dr_sem.at[h, n], sibling)

    def spread_second(h, first):
        ref = block(h, first, 0)
        for d in range(1, 4):
            send(ref, ref, as_sem.at[h, 1 + first, d], ar_sem.at[h, 1 + first, d], at(*off(h, 0, d)))
        to_sibling(h, first, 0)

    for h in range(2):
        ref = block(h, 0, 0)
        for d in range(1, 4):
            send(ref, ref, as_sem.at[h, 0, d], ar_sem.at[h, 0, d], at(*off(h, d, 0)))
    for h in range(2):
        spread_second(h, 0)
    for d in (1, 3, 2):
        for h in range(2):
            ref = block(h, 4 - d, 0)
            remote(ref, ref, as_sem.at[h, 0, d], ar_sem.at[h, 0, d], sibling).wait_recv()
            spread_second(h, 4 - d)
    for first in (0, 3, 1, 2):
        for d in (1, 3, 2):
            for h in range(2):
                ref = block(h, first, 4 - d)
                remote(ref, ref, as_sem.at[h, 1 + first, d], ar_sem.at[h, 1 + first, d], sibling).wait_recv()
                to_sibling(h, first, 4 - d)
    for n in range(16):
        for h in range(2):
            px, py = off(h, n // 4, n % 4)
            qx, gy = cell(px, py)
            ref = arrays[h][0].at[qx + 1 - 2 * c, gy]
            remote(ref, ref, ds_sem.at[h, n], dr_sem.at[h, n], sibling).wait_recv()

    route = dy[mq, :, :, pl.ds(QF, 128)].reshape(ROWS, 128).astype(F32)
    route_lane = lax.broadcasted_iota(jnp.int32, (ROWS, 128), 1)
    weight = jnp.sum(jnp.where(route_lane % 4 == ex, route, 0.0), axis=1, keepdims=True)

    for q in range(NQ):
        part = dot(tk[q].reshape(ROWS, QF), wgu[pl.ds(q * QF, QF), :])
        g[q] = (weight * dy[q, :, :, pl.ds(0, QF)].reshape(ROWS, QF).astype(F32)).astype(BF)
        back = dot(g[q], wdt[pl.ds(q * QF, QF), :])
        if q == 0:
            acts[:, pl.ds(0, 2 * HID)] = part
            acts[:, pl.ds(2 * HID, HID)] = back
        else:
            acts[:, pl.ds(0, 2 * HID)] += part
            acts[:, pl.ds(2 * HID, HID)] += back
    gate, up, dh = acts[:, pl.ds(0, HID)], acts[:, pl.ds(HID, HID)], acts[:, pl.ds(2 * HID, HID)]
    sigma = jax.nn.sigmoid(gate)
    active = gate * sigma
    hid[...] = (active * up).astype(BF)
    dcat[:, pl.ds(0, HID)] = (dh * up * (sigma + active * (1.0 - sigma))).astype(BF)
    dcat[:, pl.ds(HID, HID)] = (dh * active).astype(BF)

    for h in range(2):
        sbuf[h] = dot(dcat[...], wgut[2 * h + 1 - c]).astype(BF).reshape(NG, GROUP, QF)
        send(sbuf.at[h], rbuf.at[h], es_sem.at[h], er_sem.at[h], sibling)
    for h in range(2):
        acc[h] = dot(dcat[...], wgut[2 * h + c]).reshape(NG, GROUP, QF)
    for h in range(2):
        remote(sbuf.at[h], rbuf.at[h], es_sem.at[h], er_sem.at[h], sibling).wait_recv()
        acc[h] = acc[h] + rbuf[h].astype(F32)

    sides = ((sl1, rl1, sl2, rl2), (sr1, rr1, sr2, rr2))

    def home(h, first, second):
        px, py = off(h, first, second)
        px, py = (x + px) % NX, (y + py) % NY
        return px // 2, py * 2 + px % 2

    for d in (2, 1, 3):
        for h in range(2):
            s1, r1, _, _ = sides[h]
            for second in range(4):
                a, b = home(h, d, second)
                s1[d, second] = acc[a, b, :, pl.ds(h * HALF, HALF)].astype(BF)
            send(s1.at[d], r1.at[d], ps_sem.at[h, d], pr_sem.at[h, d], at(*off(h, d, 0)))

    for q in range(NQ):
        both = lax.dot_general(
            tk[q].reshape(ROWS, QF), dcat[...], (((0,), (0,)), ((), ())), preferred_element_type=F32
        ).astype(BF)
        gg_ref[0, pl.ds(q * QF, QF), :] = both[:, :HID]
        gu_ref[0, pl.ds(q * QF, QF), :] = both[:, HID:]
    hid_t = hid[...].T
    for q in range(NQ):
        gd_ref[0, :, pl.ds(q * QF, QF)] = dot(hid_t, g[q]).astype(BF)

    for h in range(2):
        s1, r1, s2, r2 = sides[h]
        for d in range(1, 4):
            remote(s1.at[d], r1.at[d], ps_sem.at[h, d], pr_sem.at[h, d], sibling).wait_recv()
        for second in (2, 1, 3, 0):
            a, b = home(h, 0, second)
            total = acc[a, b, :, pl.ds(h * HALF, HALF)]
            for d in range(1, 4):
                total = total + r1[d, second].astype(F32)
            if second == 0:
                acc[a, b, :, pl.ds(h * HALF, HALF)] = total
            else:
                s2[second] = total.astype(BF)
                send(s2.at[second], r2.at[second], qs_sem.at[h, second], qr_sem.at[h, second], at(*off(h, 0, second)))
    a0, b0 = home(0, 0, 0)
    for h in range(2):
        s1, r1, s2, r2 = sides[h]
        total = acc[a0, b0, :, pl.ds(h * HALF, HALF)]
        for d in range(1, 4):
            remote(s2.at[d], r2.at[d], qs_sem.at[h, d], qr_sem.at[h, d], sibling).wait_recv()
            total = total + r2[d].astype(F32)
        zsum[:, pl.ds(h * HALF, HALF)] = total.astype(BF)

    r = lax.broadcasted_iota(jnp.int32, (NZ * 16, GROUP), 0)
    s = lax.broadcasted_iota(jnp.int32, (NZ * 16, GROUP), 1)
    packed = jnp.zeros((NZ * 16, 256), F32)
    for third in range(3):
        k = r % 16 - 3 * third
        place = ((k >= 0) & (k < TOK) & (s == (r // 16) * TOK + k)).astype(F32).astype(BF)
        packed = packed + dot(place, zsum[:, pl.ds(256 * third, 256)])
    sz[...] = packed.astype(BF).reshape(NZ, 16, 256)
    for d in (8, 7, 9, 6, 10, 5, 11, 4, 12, 3, 13, 2, 14, 1, 15):
        send(sz.at[(z + d) % NZ], rz.at[d], fs_sem.at[d], fr_sem.at[d], zdev(d))
    total = sz[z].astype(F32)
    for d in range(1, NZ):
        remote(sz.at[(z + d) % NZ], rz.at[d], fs_sem.at[d], fr_sem.at[d], zdev(d)).wait_recv()
        total = total + rz[d].astype(F32)
    stage[:, pl.ds(0, 256)] = total
    for third in range(3):
        gx_ref[:, pl.ds(256 * third, 256)] = stage[pl.ds(3 * third, TOK), pl.ds(0, 256)].astype(BF)

    for copy in sends:
        copy.wait_send()


def shards(tokens, out_grad, expert_ids, gate_weights, w_gate, w_up, w_down):
    vmem = pl.BlockSpec(memory_space=pltpu.VMEM)
    anywhere = pl.BlockSpec(memory_space=pl.ANY)
    dma = pltpu.SemaphoreType.DMA
    return pl.pallas_call(
        kernel,
        out_shape=(
            jax.ShapeDtypeStruct((TOK, QF), BF),
            jax.ShapeDtypeStruct((1, D, HID), BF),
            jax.ShapeDtypeStruct((1, D, HID), BF),
            jax.ShapeDtypeStruct((1, HID, D), BF),
        ),
        in_specs=[vmem] * 4 + [anywhere] * 3,
        out_specs=(vmem,) * 4,
        scratch_shapes=[
            pltpu.VMEM((16, HALF), F32),
            pltpu.VMEM((NZ, 16, HALF), BF),
            pltpu.VMEM((NQ, NG, GROUP, QF), BF),
            pltpu.VMEM((NQ, NG, GROUP, YW), BF),
            pltpu.VMEM((NQ, ROWS, QF), BF),
            pltpu.VMEM((D, 2 * HID), BF),
            pltpu.VMEM((NQ, 2 * HID, QF), BF),
            pltpu.VMEM((HID, D), BF),
            pltpu.VMEM((D, HID), BF),
            pltpu.VMEM((ROWS, 3 * HID), F32),
            pltpu.VMEM((ROWS, 2 * HID), BF),
            pltpu.VMEM((ROWS, HID), BF),
            pltpu.VMEM((2, NG, GROUP, QF), F32),
            pltpu.VMEM((2, NG, GROUP, QF), BF),
            pltpu.VMEM((2, NG, GROUP, QF), BF),
            pltpu.VMEM((4, 4, GROUP, HALF), BF),
            pltpu.VMEM((4, 4, GROUP, HALF), BF),
            pltpu.VMEM((4, 4, GROUP, HALF), BF),
            pltpu.VMEM((4, 4, GROUP, HALF), BF),
            pltpu.VMEM((4, GROUP, HALF), BF),
            pltpu.VMEM((4, GROUP, HALF), BF),
            pltpu.VMEM((4, GROUP, HALF), BF),
            pltpu.VMEM((4, GROUP, HALF), BF),
            pltpu.VMEM((NZ, 16, 256), BF),
            pltpu.VMEM((NZ, 16, 256), BF),
            pltpu.VMEM((GROUP, QF), BF),
            dma((3,)),
            dma((NZ,)), dma((NZ,)),
            dma((2, 5, 4)), dma((2, 5, 4)),
            dma((2, 16)), dma((2, 16)),
            dma((2,)), dma((2,)),
            dma((2, 4)), dma((2, 4)),
            dma((2, 4)), dma((2, 4)),
            dma((NZ,)), dma((NZ,)),
        ],
        compiler_params=pltpu.CompilerParams(
            collective_id=0, has_side_effects=True, vmem_limit_bytes=48 * 2**20
        ),
        cost_estimate=pl.CostEstimate(flops=2_400_000_000, bytes_accessed=4_800_000, transcendentals=49152),
        name="moe_backward",
    )(tokens, out_grad, expert_ids, gate_weights, w_gate, w_up, w_down)


def solution(mesh):
    placed = (
        P("dp", "expert"),
        P("dp", "expert"),
        P("dp", None),
        P("dp", None),
        P("expert", None, "dp"),
        P("expert", None, "dp"),
        P("expert", "dp", None),
    )
    return jax.shard_map(
        shards,
        mesh=mesh,
        in_specs=placed,
        out_specs=(
            P("dp", "expert"),
            P("expert", None, "dp"),
            P("expert", None, "dp"),
            P("expert", "dp", None),
        ),
        check_vma=False,
    )
```

```python
import jax
import jax.numpy as jnp
from jax import lax
from jax.experimental import pallas as pl
from jax.experimental.pallas import tpu as pltpu
from jax.sharding import PartitionSpec as P

MESH = pl.DeviceIdType.MESH
NX, NY, NZ = 4, 4, 16
PEERS_Z = (1, 2, 3, 4, -1, -2, -3, -4)
TOK = 3
QF = 768
NQ = 4
HALF = QF // 2
GROUP = NZ * TOK
NG = 8
ROWS = NG * GROUP
HID = 128
D = NQ * QF
YW = QF + 128
WIDE = (QF, YW)
CUT = (384, 512)
BF, F32 = jnp.bfloat16, jnp.float32


def dot(a, b):
    return jnp.dot(a, b, preferred_element_type=F32)


def kernel(
    tok_ref, dy_ref, ids_ref, gw_ref, wg_hbm, wu_hbm, wd_hbm,
    gx_ref, gg_hbm, gu_hbm, gd_hbm,
    stage, zb, tk, dy, g, wgu, wgut, wd, wdt, acts, dcat, hid, acc, sbuf, rbuf,
    sl1, rl1, sr1, rr1, sl2, rl2, sr2, rr2, sz, rz, zsum, gg, gu, gd,
    w_sem, o_sem, zs_sem, zr_sem, as_sem, ar_sem, ds_sem, dr_sem, es_sem, er_sem,
    ps_sem, pr_sem, qs_sem, qr_sem, fs_sem, fr_sem,
):
    dp = lax.axis_index("dp")
    ex = lax.axis_index("expert")
    rem, div = lax.rem, lax.div
    z, xl, y = rem(dp, NZ), rem(div(dp, NZ), 2), div(dp, 2 * NZ)
    xh, c = div(ex, 2), rem(ex, 2)
    x = xh * 2 + xl

    xs = [x] + [rem(x + d, NX) for d in range(1, NX)]
    ys = [y] + [rem(y + d, NY) for d in range(1, NY)]
    zs = [z] + [rem(z + d, NZ) for d in range(1, NZ)]
    xhs, xls = [div(v, 2) for v in xs], [rem(v, 2) for v in xs]
    planes = [[(ys[j] * 2 + xls[i], xhs[i] * 2 + c) for j in range(NY)] for i in range(NX)]
    here = planes[0][0][0] * NZ
    sibling = (dp, ex + 1 - 2 * c)
    along_z = [(here + zs[d], ex) for d in range(NZ)]
    around = {(i, j): (planes[i][j][0] * NZ + z, planes[i][j][1]) for i in range(NX) for j in range(NY) if i * j == 0}

    def at(dx, dy_):
        return around[dx % NX, dy_ % NY]

    def zdev(d):
        return along_z[d % NZ]

    def cell(dx, dy_):
        group, quarter = planes[dx % NX][dy_ % NY]
        return quarter, group

    loads = [
        pltpu.make_async_copy(wg_hbm.at[0], wgu.at[:, pl.ds(0, HID)], w_sem.at[0]),
        pltpu.make_async_copy(wu_hbm.at[0], wgu.at[:, pl.ds(HID, HID)], w_sem.at[1]),
        pltpu.make_async_copy(wd_hbm.at[0], wd, w_sem.at[2]),
    ]
    for copy in loads:
        copy.start()

    barrier = pltpu.get_barrier_semaphore()
    peers = [zdev(d) for d in PEERS_Z]
    peers += [at(d, 0) for d in range(1, NX)] + [at(0, d) for d in range(1, NY)] + [sibling]
    for peer in peers:
        pl.semaphore_signal(barrier, inc=1, device_id=peer, device_id_type=MESH)

    stage[...] = jnp.zeros_like(stage)
    for i, ref in enumerate((tok_ref, dy_ref)):
        v = ref[...].astype(F32)
        stage[pl.ds(6 * i, TOK), :] = v[:, :HALF]
        stage[pl.ds(6 * i + TOK, TOK), :] = v[:, HALF:]
    lane = lax.broadcasted_iota(jnp.int32, (1, 128), 1)
    for t in range(TOK):
        w = jnp.zeros((1, 128), F32)
        for k in range(2):
            w = w + jnp.where(ids_ref[k, t] == lane % 4, gw_ref[k, t], 0.0)
        hi = w.astype(BF).astype(F32)
        mid = (w - hi).astype(BF).astype(F32)
        low = w - hi - mid
        w = jnp.where(lane < 4, hi, jnp.where(lane < 8, mid, jnp.where(lane < 12, low, 0.0)))
        stage[pl.ds(12 + t, 1), pl.ds(0, 128)] = w
    zb[z] = stage[...].astype(BF)

    pl.semaphore_wait(barrier, len(peers))

    def remote(src, dst, ssem, rsem, device):
        return pltpu.make_async_remote_copy(
            src_ref=src, dst_ref=dst, send_sem=ssem, recv_sem=rsem, device_id=device, device_id_type=MESH
        )

    sends = []

    def send(src, dst, ssem, rsem, device):
        copy = remote(src, dst, ssem, rsem, device)
        copy.start()
        sends.append(copy)

    def pass_on(origin, step, d):
        ref = zb.at[zs[origin % NZ]]
        send(ref, ref, zs_sem.at[d % NZ], zr_sem.at[d % NZ], zdev(step))

    for d in (4, -4, 2, -2, 1, -1):
        pass_on(0, d, d)

    def arrived(d):
        ref = zb.at[zs[-d % NZ]]
        remote(ref, ref, zs_sem.at[d % NZ], zr_sem.at[d % NZ], sibling).wait_recv()

    arrived(4)
    for step in (4, 3, 2, 1, -1):
        pass_on(-4, step, 4 + step)
    arrived(-4)
    for step in (-3, -2, -1, 1):
        pass_on(4, step, step - 4)
    for copy in loads:
        copy.wait()
    for q in range(NQ):
        wgut[q] = wgu[pl.ds(q * QF, QF), :].T
        wdt[pl.ds(q * QF, QF), :] = wd[:, pl.ds(q * QF, QF)].T

    for d in (1, -1, 2, -2, 3, -3, 5, -5, 6, -6, 7, -7, 8):
        arrived(d)

    r = lax.broadcasted_iota(jnp.int32, (5 * GROUP, NZ * 16), 0)
    s = lax.broadcasted_iota(jnp.int32, (5 * GROUP, NZ * 16), 1)
    k = s % 16
    kind = (k * 11) // 32
    pick = ((r == kind * GROUP + (s // 16) * TOK + (k - 3 * kind)) & (k < 15)).astype(F32).astype(BF)
    rows = dot(pick, zb[...].reshape(NZ * 16, HALF)).astype(BF)
    mq, mg = cell(0, 0)
    tk[mq, mg, :, pl.ds(0, HALF)] = rows[0:GROUP]
    tk[mq, mg, :, pl.ds(HALF, HALF)] = rows[GROUP : 2 * GROUP]
    dy[mq, mg, :, pl.ds(0, HALF)] = rows[2 * GROUP : 3 * GROUP]
    dy[mq, mg, :, pl.ds(HALF, HALF)] = rows[3 * GROUP : 4 * GROUP]
    dy[mq, mg, :, pl.ds(QF, 128)] = rows[4 * GROUP : 5 * GROUP, 0:128]

    arrays = ((tk, 0), (dy, 1))

    def off(h, first, second):
        return (first, second) if h == 0 else (second, first)

    def block(h, first, second, part=None):
        q_, g_ = cell(*off(h, first, second))
        if part is None:
            return arrays[h][0].at[q_, g_]
        return arrays[h][0].at[q_, g_, :, pl.ds(*((0, CUT[h]) if part == 0 else (CUT[h], WIDE[h] - CUT[h])))]

    def to_sibling(h, first, second):
        ref = block(h, first, second)
        n = (first % 4) * 4 + second % 4
        send(ref, ref, ds_sem.at[h, n], dr_sem.at[h, n], sibling)

    def spot(first, d):
        return (d, 0) if first is None else (first, d)

    def sems(h, first, kind):
        n = 0 if first is None else 1 + first % 4
        return as_sem.at[h, n, kind], ar_sem.at[h, n, kind]

    def to_next(h, first, d, step, kind, part=None):
        ref = block(h, *spot(first, d), part)
        send(ref, ref, *sems(h, first, kind), at(*off(h, *((step, 0) if first is None else (0, step)))))

    def both_ways(h, first):
        to_next(h, first, 0, 1, 0)
        to_next(h, first, 0, -1, 1)

    def wait_near(h, first, kind):
        d = -1 if kind == 0 else 1
        ref = block(h, *spot(first, d))
        remote(ref, ref, *sems(h, first, kind), sibling).wait_recv()
        to_next(h, first, d, -d, 2 + kind, kind)

    def wait_far(h, first):
        for part in range(2):
            ref = block(h, *spot(first, 2), part)
            remote(ref, ref, *sems(h, first, 2 + part), sibling).wait_recv()

    for h in range(2):
        both_ways(h, None)
    for h in range(2):
        both_ways(h, 0)
    for h in range(2):
        to_sibling(h, 0, 0)
    for kind in range(2):
        for h in range(2):
            wait_near(h, None, kind)
            both_ways(h, 2 * kind - 1)
            to_sibling(h, 2 * kind - 1, 0)
    for kind in range(2):
        for h in range(2):
            wait_near(h, 0, kind)
            to_sibling(h, 0, 2 * kind - 1)
    for h in range(2):
        wait_far(h, None)
        both_ways(h, 2)
        to_sibling(h, 2, 0)
    for first in (-1, 1, 2):
        for kind in range(2):
            for h in range(2):
                wait_near(h, first, kind)
                to_sibling(h, first, 2 * kind - 1)
    for first in (0, -1, 1, 2):
        for h in range(2):
            wait_far(h, first)
            to_sibling(h, first, 2)
    for n in range(16):
        for h in range(2):
            px, py = off(h, n // 4, n % 4)
            qx, gy = cell(px, py)
            ref = arrays[h][0].at[qx + 1 - 2 * c, gy]
            remote(ref, ref, ds_sem.at[h, n], dr_sem.at[h, n], sibling).wait_recv()

    route = dy[mq, :, :, pl.ds(QF, 128)].reshape(ROWS, 128).astype(F32)
    route_lane = lax.broadcasted_iota(jnp.int32, (ROWS, 128), 1)
    weight = jnp.sum(jnp.where(route_lane % 4 == ex, route, 0.0), axis=1, keepdims=True)

    for q in range(NQ):
        part = dot(tk[q].reshape(ROWS, QF), wgu[pl.ds(q * QF, QF), :])
        g[q] = (weight * dy[q, :, :, pl.ds(0, QF)].reshape(ROWS, QF).astype(F32)).astype(BF)
        back = dot(g[q], wdt[pl.ds(q * QF, QF), :])
        if q == 0:
            acts[:, pl.ds(0, 2 * HID)] = part
            acts[:, pl.ds(2 * HID, HID)] = back
        else:
            acts[:, pl.ds(0, 2 * HID)] += part
            acts[:, pl.ds(2 * HID, HID)] += back
    gate, up, dh = acts[:, pl.ds(0, HID)], acts[:, pl.ds(HID, HID)], acts[:, pl.ds(2 * HID, HID)]
    sigma = jax.nn.sigmoid(gate)
    active = gate * sigma
    hid[...] = (active * up).astype(BF)
    dcat[:, pl.ds(0, HID)] = (dh * up * (sigma + active * (1.0 - sigma))).astype(BF)
    dcat[:, pl.ds(HID, HID)] = (dh * active).astype(BF)

    for h in range(2):
        sbuf[h] = dot(dcat[...], wgut[2 * h + 1 - c]).astype(BF).reshape(NG, GROUP, QF)
        send(sbuf.at[h], rbuf.at[h], es_sem.at[h], er_sem.at[h], sibling)
    for h in range(2):
        acc[h] = dot(dcat[...], wgut[2 * h + c]).reshape(NG, GROUP, QF)
    for h in range(2):
        remote(sbuf.at[h], rbuf.at[h], es_sem.at[h], er_sem.at[h], sibling).wait_recv()
        acc[h] = acc[h] + rbuf[h].astype(F32)

    sides = ((sl1, rl1, sl2, rl2), (sr1, rr1, sr2, rr2))

    def home(h, first, second):
        px, py = off(h, first, second)
        return xhs[px], planes[px][py][0]

    for d in (2, 1, 3):
        for h in range(2):
            s1, r1, _, _ = sides[h]
            for second in range(4):
                a, b = home(h, d, second)
                s1[d, second] = acc[a, b, :, pl.ds(h * HALF, HALF)].astype(BF)
            send(s1.at[d], r1.at[d], ps_sem.at[h, d], pr_sem.at[h, d], at(*off(h, d, 0)))

    for q in range(NQ):
        both = lax.dot_general(
            tk[q].reshape(ROWS, QF), dcat[...], (((0,), (0,)), ((), ())), preferred_element_type=F32
        ).astype(BF)
        gg[pl.ds(q * QF, QF), :] = both[:, :HID]
        gu[pl.ds(q * QF, QF), :] = both[:, HID:]
    hid_t = hid[...].T
    for q in range(NQ):
        gd[:, pl.ds(q * QF, QF)] = dot(hid_t, g[q]).astype(BF)
    stores = [
        pltpu.make_async_copy(gg, gg_hbm.at[0], o_sem.at[0]),
        pltpu.make_async_copy(gu, gu_hbm.at[0], o_sem.at[1]),
        pltpu.make_async_copy(gd, gd_hbm.at[0], o_sem.at[2]),
    ]
    for copy in stores:
        copy.start()

    for h in range(2):
        s1, r1, s2, r2 = sides[h]
        for d in range(1, 4):
            remote(s1.at[d], r1.at[d], ps_sem.at[h, d], pr_sem.at[h, d], sibling).wait_recv()
        for second in (2, 1, 3, 0):
            a, b = home(h, 0, second)
            total = acc[a, b, :, pl.ds(h * HALF, HALF)]
            for d in range(1, 4):
                total = total + r1[d, second].astype(F32)
            if second == 0:
                acc[a, b, :, pl.ds(h * HALF, HALF)] = total
            else:
                s2[second] = total.astype(BF)
                send(s2.at[second], r2.at[second], qs_sem.at[h, second], qr_sem.at[h, second], at(*off(h, 0, second)))
    a0, b0 = home(0, 0, 0)
    for h in range(2):
        s1, r1, s2, r2 = sides[h]
        total = acc[a0, b0, :, pl.ds(h * HALF, HALF)]
        for d in range(1, 4):
            remote(s2.at[d], r2.at[d], qs_sem.at[h, d], qr_sem.at[h, d], sibling).wait_recv()
            total = total + r2[d].astype(F32)
        zsum[:, pl.ds(h * HALF, HALF)] = total.astype(BF)

    r = lax.broadcasted_iota(jnp.int32, (NZ * 16, GROUP), 0)
    s = lax.broadcasted_iota(jnp.int32, (NZ * 16, GROUP), 1)
    packed = jnp.zeros((NZ * 16, 256), F32)
    for third in range(3):
        k = r % 16 - 3 * third
        place = ((k >= 0) & (k < TOK) & (s == (r // 16) * TOK + k)).astype(F32).astype(BF)
        packed = packed + dot(place, zsum[:, pl.ds(256 * third, 256)])
    sz[...] = packed.astype(BF).reshape(NZ, 16, 256)
    def hand_in(step, d):
        send(sz.at[zs[d % NZ]], rz.at[-d % NZ], fs_sem.at[-d % NZ], fr_sem.at[-d % NZ], zdev(step))

    def handed(d):
        remote(sz.at[z], rz.at[d % NZ], fs_sem.at[d % NZ], fr_sem.at[d % NZ], sibling).wait_recv()
        return rz[d % NZ].astype(F32)

    for far in (8, 7, 6, 5, 3):
        hand_in(4 - far, -far)
    for far in (7, 6, 5, 3):
        hand_in(far - 4, far)
    for d in (1, -1, 2, -2):
        hand_in(d, d)
    for hub, fars in ((4, (3, 5, 6, 7, 8)), (-4, (-3, -5, -6, -7))):
        ref = sz.at[zs[-hub % NZ]]
        total = ref[...].astype(F32)
        for far in fars:
            total = total + handed(far)
        ref[...] = total.astype(BF)
        hand_in(-hub, -hub)
    total = sz[z].astype(F32)
    for d in (1, -1, 2, -2, 4, -4):
        total = total + handed(d)
    stage[:, pl.ds(0, 256)] = total
    for third in range(3):
        gx_ref[:, pl.ds(256 * third, 256)] = stage[pl.ds(3 * third, TOK), pl.ds(0, 256)].astype(BF)

    for copy in stores:
        copy.wait()
    for copy in sends:
        copy.wait_send()


def settle(gx_in, gg_in, gu_in, gd_in, gx, gg, gu, gd, bg, bu, bd, in_sem, out_sem):
    gx[...] = gx_in[...]
    moves = []
    for i, (src, via, dst) in enumerate(((gg_in, bg, gg), (gu_in, bu, gu), (gd_in, bd, gd))):
        half = via.shape[0] // 2
        for j in range(2):
            part = pl.ds(j * half, half)
            moves.append((
                pltpu.make_async_copy(src.at[0, part], via.at[part], in_sem.at[i, j]),
                pltpu.make_async_copy(via.at[part], dst.at[0, part], out_sem.at[i, j]),
            ))
    for come, _ in moves:
        come.start()
    for come, go in moves:
        come.wait()
        go.start()
    for _, go in moves:
        go.wait()


def shards(tokens, out_grad, expert_ids, gate_weights, w_gate, w_up, w_down):
    vmem = pl.BlockSpec(memory_space=pltpu.VMEM)
    anywhere = pl.BlockSpec(memory_space=pl.ANY)
    smem = pl.BlockSpec(memory_space=pltpu.SMEM)
    dma = pltpu.SemaphoreType.DMA
    results = pl.pallas_call(
        kernel,
        out_shape=(
            jax.ShapeDtypeStruct((TOK, QF), BF),
            jax.ShapeDtypeStruct((1, D, HID), BF),
            jax.ShapeDtypeStruct((1, D, HID), BF),
            jax.ShapeDtypeStruct((1, HID, D), BF),
        ),
        in_specs=[vmem] * 2 + [smem] * 2 + [anywhere] * 3,
        out_specs=(vmem,) + (anywhere,) * 3,
        scratch_shapes=[
            pltpu.VMEM((16, HALF), F32),
            pltpu.VMEM((NZ, 16, HALF), BF),
            pltpu.VMEM((NQ, NG, GROUP, QF), BF),
            pltpu.VMEM((NQ, NG, GROUP, YW), BF),
            pltpu.VMEM((NQ, ROWS, QF), BF),
            pltpu.VMEM((D, 2 * HID), BF),
            pltpu.VMEM((NQ, 2 * HID, QF), BF),
            pltpu.VMEM((HID, D), BF),
            pltpu.VMEM((D, HID), BF),
            pltpu.VMEM((ROWS, 3 * HID), F32),
            pltpu.VMEM((ROWS, 2 * HID), BF),
            pltpu.VMEM((ROWS, HID), BF),
            pltpu.VMEM((2, NG, GROUP, QF), F32),
            pltpu.VMEM((2, NG, GROUP, QF), BF),
            pltpu.VMEM((2, NG, GROUP, QF), BF),
            pltpu.VMEM((4, 4, GROUP, HALF), BF),
            pltpu.VMEM((4, 4, GROUP, HALF), BF),
            pltpu.VMEM((4, 4, GROUP, HALF), BF),
            pltpu.VMEM((4, 4, GROUP, HALF), BF),
            pltpu.VMEM((4, GROUP, HALF), BF),
            pltpu.VMEM((4, GROUP, HALF), BF),
            pltpu.VMEM((4, GROUP, HALF), BF),
            pltpu.VMEM((4, GROUP, HALF), BF),
            pltpu.VMEM((NZ, 16, 256), BF),
            pltpu.VMEM((NZ, 16, 256), BF),
            pltpu.VMEM((GROUP, QF), BF),
            pltpu.VMEM((D, HID), BF),
            pltpu.VMEM((D, HID), BF),
            pltpu.VMEM((HID, D), BF),
            dma((3,)), dma((3,)),
            dma((NZ,)), dma((NZ,)),
            dma((2, 5, 4)), dma((2, 5, 4)),
            dma((2, 16)), dma((2, 16)),
            dma((2,)), dma((2,)),
            dma((2, 4)), dma((2, 4)),
            dma((2, 4)), dma((2, 4)),
            dma((NZ,)), dma((NZ,)),
        ],
        compiler_params=pltpu.CompilerParams(
            collective_id=0, has_side_effects=True, vmem_limit_bytes=60 * 2**20
        ),
        cost_estimate=pl.CostEstimate(flops=2_400_000_000, bytes_accessed=4_800_000, transcendentals=49152),
        name="moe_backward",
    )(tokens, out_grad, expert_ids.T, gate_weights.T, w_gate, w_up, w_down)
    return pl.pallas_call(
        settle,
        out_shape=[jax.ShapeDtypeStruct(v.shape, v.dtype) for v in results],
        in_specs=[vmem] + [anywhere] * 3,
        out_specs=[vmem] + [anywhere] * 3,
        scratch_shapes=[
            pltpu.VMEM((D, HID), BF),
            pltpu.VMEM((D, HID), BF),
            pltpu.VMEM((HID, D), BF),
            dma((3, 2)), dma((3, 2)),
        ],
        compiler_params=pltpu.CompilerParams(vmem_limit_bytes=60 * 2**20),
        name="settle",
    )(*results)


def solution(mesh):
    placed = (
        P("dp", "expert"),
        P("dp", "expert"),
        P("dp", None),
        P("dp", None),
        P("expert", None, "dp"),
        P("expert", None, "dp"),
        P("expert", "dp", None),
    )
    return jax.shard_map(
        shards,
        mesh=mesh,
        in_specs=placed,
        out_specs=(
            P("dp", "expert"),
            P("expert", None, "dp"),
            P("expert", None, "dp"),
            P("expert", "dp", None),
        ),
        check_vma=False,
    )
```

```python
import jax
import jax.numpy as jnp
from jax import lax
from jax.experimental import pallas as pl
from jax.experimental.pallas import tpu as pltpu
from jax.sharding import PartitionSpec as P

MESH = pl.DeviceIdType.MESH
NX, NY, NZ = 4, 4, 16
PEERS_Z = (1, 2, 3, 4, -1, -2, -3, -4)
TOK = 3
QF = 768
NQ = 4
HALF = QF // 2
GROUP = NZ * TOK
NG = 8
ROWS = NG * GROUP
HID = 128
D = NQ * QF
YW = QF + 128
WIDE = (QF, YW)
CUT = (384, 512)
BF, F32 = jnp.bfloat16, jnp.float32


def dot(a, b):
    return jnp.dot(a, b, preferred_element_type=F32)


def kernel(
    tok_ref, dy_ref, ids_ref, gw_ref, wg_hbm, wu_hbm, wd_hbm,
    gx_ref, gg_ref, gu_ref, gd_ref,
    stage, zb, tk, dy, g, wgu, wgut, wd, wdt, acts, dcat, hid, acc, sbuf, rbuf,
    sl1, rl1, sr1, rr1, sl2, rl2, sr2, rr2, sz, rz, zsum, mine,
    w_sem, zs_sem, zr_sem, as_sem, ar_sem, ds_sem, dr_sem, es_sem, er_sem,
    ps_sem, pr_sem, qs_sem, qr_sem, fs_sem, fr_sem,
):
    dp = lax.axis_index("dp")
    ex = lax.axis_index("expert")
    rem, div = lax.rem, lax.div
    z, xl, y = rem(dp, NZ), rem(div(dp, NZ), 2), div(dp, 2 * NZ)
    xh, c = div(ex, 2), rem(ex, 2)
    x = xh * 2 + xl

    xs = [x] + [rem(x + d, NX) for d in range(1, NX)]
    ys = [y] + [rem(y + d, NY) for d in range(1, NY)]
    zs = [z] + [rem(z + d, NZ) for d in range(1, NZ)]
    xhs, xls = [div(v, 2) for v in xs], [rem(v, 2) for v in xs]
    planes = [[(ys[j] * 2 + xls[i], xhs[i] * 2 + c) for j in range(NY)] for i in range(NX)]
    here = planes[0][0][0] * NZ
    sibling = (dp, ex + 1 - 2 * c)
    along_z = [(here + zs[d], ex) for d in range(NZ)]
    around = {(i, j): (planes[i][j][0] * NZ + z, planes[i][j][1]) for i in range(NX) for j in range(NY) if i * j == 0}

    def at(dx, dy_):
        return around[dx % NX, dy_ % NY]

    def zdev(d):
        return along_z[d % NZ]

    def cell(dx, dy_):
        group, quarter = planes[dx % NX][dy_ % NY]
        return quarter, group

    loads = [pltpu.make_async_copy(wd_hbm.at[0], wd, w_sem.at[2 * NQ])]
    for q in range(NQ):
        for i, ref in enumerate((wg_hbm, wu_hbm)):
            part = ref.at[0, pl.ds(q * QF, QF)]
            loads.append(pltpu.make_async_copy(part, wgu.at[q, :, pl.ds(i * HID, HID)], w_sem.at[2 * q + i]))
    for copy in loads:
        copy.start()

    barrier = pltpu.get_barrier_semaphore()
    peers = [zdev(d) for d in PEERS_Z]
    peers += [at(d, 0) for d in range(1, NX)] + [at(0, d) for d in range(1, NY)] + [sibling]
    for peer in peers:
        pl.semaphore_signal(barrier, inc=1, device_id=peer, device_id_type=MESH)

    stage[...] = jnp.zeros_like(stage)
    for i, ref in enumerate((tok_ref, dy_ref)):
        v = ref[...].astype(F32)
        stage[pl.ds(6 * i, TOK), :] = v[:, :HALF]
        stage[pl.ds(6 * i + TOK, TOK), :] = v[:, HALF:]
    lane = lax.broadcasted_iota(jnp.int32, (1, 128), 1)
    for t in range(TOK):
        w = jnp.zeros((1, 128), F32)
        for k in range(2):
            w = w + jnp.where(ids_ref[k, t] == lane % 4, gw_ref[k, t], 0.0)
        hi = w.astype(BF).astype(F32)
        mid = (w - hi).astype(BF).astype(F32)
        low = w - hi - mid
        w = jnp.where(lane < 4, hi, jnp.where(lane < 8, mid, jnp.where(lane < 12, low, 0.0)))
        stage[pl.ds(12 + t, 1), pl.ds(0, 128)] = w
    zb[z] = stage[...].astype(BF)

    pl.semaphore_wait(barrier, len(peers))

    def remote(src, dst, ssem, rsem, device):
        return pltpu.make_async_remote_copy(
            src_ref=src, dst_ref=dst, send_sem=ssem, recv_sem=rsem, device_id=device, device_id_type=MESH
        )

    sends = []

    def send(src, dst, ssem, rsem, device):
        copy = remote(src, dst, ssem, rsem, device)
        copy.start()
        sends.append(copy)

    def pass_on(origin, step, d):
        ref = zb.at[zs[origin % NZ]]
        send(ref, ref, zs_sem.at[d % NZ], zr_sem.at[d % NZ], zdev(step))

    for d in (4, -4, 2, -2, 1, -1):
        pass_on(0, d, d)

    def arrived(d):
        ref = zb.at[zs[-d % NZ]]
        remote(ref, ref, zs_sem.at[d % NZ], zr_sem.at[d % NZ], sibling).wait_recv()

    arrived(4)
    for step in (4, 3, 2, 1, -1):
        pass_on(-4, step, 4 + step)
    arrived(-4)
    for step in (-3, -2, -1, 1):
        pass_on(4, step, step - 4)
    for copy in loads:
        copy.wait()
    for q in range(NQ):
        wgut[q] = wgu[q].T
        wdt[q] = wd[:, pl.ds(q * QF, QF)].T

    for d in (1, -1, 2, -2, 3, -3, 5, -5, 6, -6, 7, -7, 8):
        arrived(d)

    r = lax.broadcasted_iota(jnp.int32, (5 * GROUP, NZ * 16), 0)
    s = lax.broadcasted_iota(jnp.int32, (5 * GROUP, NZ * 16), 1)
    k = s % 16
    kind = (k * 11) // 32
    pick = ((r == kind * GROUP + (s // 16) * TOK + (k - 3 * kind)) & (k < 15)).astype(F32).astype(BF)
    rows = dot(pick, zb[...].reshape(NZ * 16, HALF)).astype(BF)
    mq, mg = cell(0, 0)
    tk[mq, mg, :, pl.ds(0, HALF)] = rows[0:GROUP]
    tk[mq, mg, :, pl.ds(HALF, HALF)] = rows[GROUP : 2 * GROUP]
    dy[mq, mg, :, pl.ds(0, HALF)] = rows[2 * GROUP : 3 * GROUP]
    dy[mq, mg, :, pl.ds(HALF, HALF)] = rows[3 * GROUP : 4 * GROUP]
    dy[mq, mg, :, pl.ds(QF, 128)] = rows[4 * GROUP : 5 * GROUP, 0:128]

    arrays = ((tk, 0), (dy, 1))

    def off(h, first, second):
        return (first, second) if h == 0 else (second, first)

    def block(h, first, second, part=None):
        q_, g_ = cell(*off(h, first, second))
        if part is None:
            return arrays[h][0].at[q_, g_]
        return arrays[h][0].at[q_, g_, :, pl.ds(*((0, CUT[h]) if part == 0 else (CUT[h], WIDE[h] - CUT[h])))]

    def to_sibling(h, first, second):
        ref = block(h, first, second)
        n = (first % 4) * 4 + second % 4
        send(ref, ref, ds_sem.at[h, n], dr_sem.at[h, n], sibling)

    def spot(first, d):
        return (d, 0) if first is None else (first, d)

    def sems(h, first, kind):
        n = 0 if first is None else 1 + first % 4
        return as_sem.at[h, n, kind], ar_sem.at[h, n, kind]

    def to_next(h, first, d, step, kind, part=None):
        ref = block(h, *spot(first, d), part)
        send(ref, ref, *sems(h, first, kind), at(*off(h, *((step, 0) if first is None else (0, step)))))

    def both_ways(h, first):
        to_next(h, first, 0, 1, 0)
        to_next(h, first, 0, -1, 1)

    def wait_near(h, first, kind):
        d = -1 if kind == 0 else 1
        ref = block(h, *spot(first, d))
        remote(ref, ref, *sems(h, first, kind), sibling).wait_recv()
        to_next(h, first, d, -d, 2 + kind, kind)

    def wait_far(h, first):
        for part in range(2):
            ref = block(h, *spot(first, 2), part)
            remote(ref, ref, *sems(h, first, 2 + part), sibling).wait_recv()

    for h in range(2):
        both_ways(h, None)
    for h in range(2):
        both_ways(h, 0)
    for h in range(2):
        to_sibling(h, 0, 0)
    for kind in range(2):
        for h in range(2):
            wait_near(h, None, kind)
            both_ways(h, 2 * kind - 1)
            to_sibling(h, 2 * kind - 1, 0)
    for kind in range(2):
        for h in range(2):
            wait_near(h, 0, kind)
            to_sibling(h, 0, 2 * kind - 1)
    for h in range(2):
        wait_far(h, None)
        both_ways(h, 2)
        to_sibling(h, 2, 0)
    for first in (-1, 1, 2):
        for kind in range(2):
            for h in range(2):
                wait_near(h, first, kind)
                to_sibling(h, first, 2 * kind - 1)
    for first in (0, -1, 1, 2):
        for h in range(2):
            wait_far(h, first)
            to_sibling(h, first, 2)
    route = dy[mq, :, :, pl.ds(QF, 128)].reshape(ROWS, 128).astype(F32)
    route_lane = lax.broadcasted_iota(jnp.int32, (ROWS, 128), 1)
    weight = jnp.sum(jnp.where(route_lane % 4 == ex, route, 0.0), axis=1, keepdims=True)

    def forward(q, fresh):
        part = dot(tk[q].reshape(ROWS, QF), wgu[q])
        g[q] = (weight * dy[q, :, :, pl.ds(0, QF)].reshape(ROWS, QF).astype(F32)).astype(BF)
        back = dot(g[q], wdt[q])
        if fresh:
            acts[:, pl.ds(0, 2 * HID)] = part
            acts[:, pl.ds(2 * HID, HID)] = back
        else:
            acts[:, pl.ds(0, 2 * HID)] += part
            acts[:, pl.ds(2 * HID, HID)] += back

    forward(c, True)
    forward(2 + c, False)
    for n in range(16):
        for h in range(2):
            px, py = off(h, n // 4, n % 4)
            qx, gy = cell(px, py)
            ref = arrays[h][0].at[qx + 1 - 2 * c, gy]
            remote(ref, ref, ds_sem.at[h, n], dr_sem.at[h, n], sibling).wait_recv()
    forward(1 - c, False)
    forward(3 - c, False)
    gate, up, dh = acts[:, pl.ds(0, HID)], acts[:, pl.ds(HID, HID)], acts[:, pl.ds(2 * HID, HID)]
    sigma = jax.nn.sigmoid(gate)
    active = gate * sigma
    hid[...] = (active * up).astype(BF)
    dcat[:, pl.ds(0, HID)] = (dh * up * (sigma + active * (1.0 - sigma))).astype(BF)
    dcat[:, pl.ds(HID, HID)] = (dh * active).astype(BF)

    sides = ((sl1, rl1, sl2, rl2), (sr1, rr1, sr2, rr2))

    def home(h, first, second):
        px, py = off(h, first, second)
        return xhs[px], planes[px][py][0]

    def both_cores(h, first, second):
        a, b = home(h, first, second)
        cols = pl.ds(h * HALF, HALF)
        return acc[a, b, :, cols] + rbuf[a, b, :, cols].astype(F32)

    def first_line(h, d):
        s1, r1, _, _ = sides[h]
        for second in range(4):
            s1[d, second] = both_cores(h, d, second).astype(BF)
        send(s1.at[d], r1.at[d], ps_sem.at[h, d], pr_sem.at[h, d], at(*off(h, d, 0)))

    near, far = xh, 1 - xh
    for i, a in enumerate((far, near)):
        sbuf[a] = dot(dcat[...], wgut[2 * a + 1 - c]).astype(BF).reshape(NG, GROUP, QF)
        send(sbuf.at[a], rbuf.at[a], es_sem.at[i], er_sem.at[i], sibling)
    for i, a in enumerate((far, near)):
        acc[a] = dot(dcat[...], wgut[2 * a + c]).reshape(NG, GROUP, QF)
        remote(sbuf.at[a], rbuf.at[a], es_sem.at[i], er_sem.at[i], sibling).wait_recv()
        if i == 0:
            first_line(0, 2)
    for h, d in ((1, 2), (0, 1), (1, 1), (0, 3), (1, 3)):
        first_line(h, d)

    for q in range(NQ):
        both = lax.dot_general(
            tk[q].reshape(ROWS, QF), dcat[...], (((0,), (0,)), ((), ())), preferred_element_type=F32
        ).astype(BF)
        gg_ref[0, pl.ds(q * QF, QF), :] = both[:, :HID]
        gu_ref[0, pl.ds(q * QF, QF), :] = both[:, HID:]
    hid_t = hid[...].T
    for q in range(NQ):
        gd_ref[0, :, pl.ds(q * QF, QF)] = dot(hid_t, g[q]).astype(BF)

    for h in range(2):
        s1, r1, s2, r2 = sides[h]
        for d in range(1, 4):
            remote(s1.at[d], r1.at[d], ps_sem.at[h, d], pr_sem.at[h, d], sibling).wait_recv()
        for second in (2, 1, 3, 0):
            total = both_cores(h, 0, second)
            for d in range(1, 4):
                total = total + r1[d, second].astype(F32)
            if second == 0:
                mine[:, pl.ds(h * HALF, HALF)] = total
            else:
                s2[second] = total.astype(BF)
                send(s2.at[second], r2.at[second], qs_sem.at[h, second], qr_sem.at[h, second], at(*off(h, 0, second)))
    for h in range(2):
        s1, r1, s2, r2 = sides[h]
        total = mine[:, pl.ds(h * HALF, HALF)]
        for d in range(1, 4):
            remote(s2.at[d], r2.at[d], qs_sem.at[h, d], qr_sem.at[h, d], sibling).wait_recv()
            total = total + r2[d].astype(F32)
        zsum[:, pl.ds(h * HALF, HALF)] = total.astype(BF)

    r = lax.broadcasted_iota(jnp.int32, (NZ * 16, GROUP), 0)
    s = lax.broadcasted_iota(jnp.int32, (NZ * 16, GROUP), 1)
    packed = jnp.zeros((NZ * 16, 256), F32)
    for third in range(3):
        k = r % 16 - 3 * third
        place = ((k >= 0) & (k < TOK) & (s == (r // 16) * TOK + k)).astype(F32).astype(BF)
        packed = packed + dot(place, zsum[:, pl.ds(256 * third, 256)])
    sz[...] = packed.astype(BF).reshape(NZ, 16, 256)
    def hand_in(step, d):
        send(sz.at[zs[d % NZ]], rz.at[-d % NZ], fs_sem.at[-d % NZ], fr_sem.at[-d % NZ], zdev(step))

    def handed(d):
        remote(sz.at[z], rz.at[d % NZ], fs_sem.at[d % NZ], fr_sem.at[d % NZ], sibling).wait_recv()
        return rz[d % NZ].astype(F32)

    for far in (8, 7, 6, 5, 3):
        hand_in(4 - far, -far)
    for far in (7, 6, 5, 3):
        hand_in(far - 4, far)
    for d in (1, -1, 2, -2):
        hand_in(d, d)
    for hub, fars in ((4, (3, 5, 6, 7, 8)), (-4, (-3, -5, -6, -7))):
        ref = sz.at[zs[-hub % NZ]]
        total = ref[...].astype(F32)
        for far in fars:
            total = total + handed(far)
        ref[...] = total.astype(BF)
        hand_in(-hub, -hub)
    total = sz[z].astype(F32)
    for d in (1, -1, 2, -2, 4, -4):
        total = total + handed(d)
    stage[:, pl.ds(0, 256)] = total
    for third in range(3):
        gx_ref[:, pl.ds(256 * third, 256)] = stage[pl.ds(3 * third, TOK), pl.ds(0, 256)].astype(BF)

    for copy in sends:
        copy.wait_send()


def settle(*refs):
    copies = [pltpu.make_async_copy(refs[i], refs[4 + i], refs[8].at[i]) for i in range(4)]
    for copy in copies:
        copy.start()
    for copy in copies:
        copy.wait()


def shards(tokens, out_grad, expert_ids, gate_weights, w_gate, w_up, w_down):
    vmem = pl.BlockSpec(memory_space=pltpu.VMEM)
    anywhere = pl.BlockSpec(memory_space=pl.ANY)
    smem = pl.BlockSpec(memory_space=pltpu.SMEM)
    dma = pltpu.SemaphoreType.DMA
    results = pl.pallas_call(
        kernel,
        out_shape=(
            pltpu.VMEM((TOK, QF), BF),
            pltpu.VMEM((1, D, HID), BF),
            pltpu.VMEM((1, D, HID), BF),
            pltpu.VMEM((1, HID, D), BF),
        ),
        in_specs=[vmem] * 2 + [smem] * 2 + [anywhere] * 3,
        out_specs=(vmem,) * 4,
        scratch_shapes=[
            pltpu.VMEM((16, HALF), F32),
            pltpu.VMEM((NZ, 16, HALF), BF),
            pltpu.VMEM((NQ, NG, GROUP, QF), BF),
            pltpu.VMEM((NQ, NG, GROUP, YW), BF),
            pltpu.VMEM((NQ, ROWS, QF), BF),
            pltpu.VMEM((NQ, QF, 2 * HID), BF),
            pltpu.VMEM((NQ, 2 * HID, QF), BF),
            pltpu.VMEM((HID, D), BF),
            pltpu.VMEM((NQ, QF, HID), BF),
            pltpu.VMEM((ROWS, 3 * HID), F32),
            pltpu.VMEM((ROWS, 2 * HID), BF),
            pltpu.VMEM((ROWS, HID), BF),
            pltpu.VMEM((2, NG, GROUP, QF), F32),
            pltpu.VMEM((2, NG, GROUP, QF), BF),
            pltpu.VMEM((2, NG, GROUP, QF), BF),
            pltpu.VMEM((4, 4, GROUP, HALF), BF),
            pltpu.VMEM((4, 4, GROUP, HALF), BF),
            pltpu.VMEM((4, 4, GROUP, HALF), BF),
            pltpu.VMEM((4, 4, GROUP, HALF), BF),
            pltpu.VMEM((4, GROUP, HALF), BF),
            pltpu.VMEM((4, GROUP, HALF), BF),
            pltpu.VMEM((4, GROUP, HALF), BF),
            pltpu.VMEM((4, GROUP, HALF), BF),
            pltpu.VMEM((NZ, 16, 256), BF),
            pltpu.VMEM((NZ, 16, 256), BF),
            pltpu.VMEM((GROUP, QF), BF),
            pltpu.VMEM((GROUP, QF), F32),
            dma((2 * NQ + 1,)),
            dma((NZ,)), dma((NZ,)),
            dma((2, 5, 4)), dma((2, 5, 4)),
            dma((2, 16)), dma((2, 16)),
            dma((2,)), dma((2,)),
            dma((2, 4)), dma((2, 4)),
            dma((2, 4)), dma((2, 4)),
            dma((NZ,)), dma((NZ,)),
        ],
        compiler_params=pltpu.CompilerParams(
            collective_id=0, has_side_effects=True, vmem_limit_bytes=56 * 2**20
        ),
        cost_estimate=pl.CostEstimate(flops=2_400_000_000, bytes_accessed=4_800_000, transcendentals=49152),
        name="moe_backward",
    )(tokens, out_grad, expert_ids.T, gate_weights.T, w_gate, w_up, w_down)
    return pl.pallas_call(
        settle,
        out_shape=[jax.ShapeDtypeStruct(v.shape, v.dtype) for v in results],
        in_specs=[anywhere] * 4,
        out_specs=[anywhere] * 4,
        scratch_shapes=[dma((4,))],
        compiler_params=pltpu.CompilerParams(vmem_limit_bytes=2**20),
        name="settle",
    )(*results)


def solution(mesh):
    placed = (
        P("dp", "expert"),
        P("dp", "expert"),
        P("dp", None),
        P("dp", None),
        P("expert", None, "dp"),
        P("expert", None, "dp"),
        P("expert", "dp", None),
    )
    return jax.shard_map(
        shards,
        mesh=mesh,
        in_specs=placed,
        out_specs=(
            P("dp", "expert"),
            P("expert", None, "dp"),
            P("expert", None, "dp"),
            P("expert", "dp", None),
        ),
        check_vma=False,
    )
```

```python
import jax
import jax.numpy as jnp
from jax import lax
from jax.experimental import pallas as pl
from jax.experimental.pallas import tpu as pltpu
from jax.sharding import PartitionSpec as P

MESH = pl.DeviceIdType.MESH
NX, NY, NZ = 4, 4, 16
PEERS_Z = (1, 2, 3, 4, -1, -2, -3, -4)
TOK = 3
QF = 768
NQ = 4
HALF = QF // 2
GROUP = NZ * TOK
NG = 8
ROWS = NG * GROUP
HID = 128
D = NQ * QF
BF, F32 = jnp.bfloat16, jnp.float32


def dot(a, b):
    return jnp.dot(a, b, preferred_element_type=F32)


def kernel(
    tok_hbm, dy_hbm, ids_hbm, gw_hbm, wg_hbm, wu_hbm, wd_hbm,
    gx_ref, gg_ref, gu_ref, gd_ref,
    tok_ref, dy_ref, ids_ref, gw_ref, stage, zb, tk, dy, rt, g, wgu, wgut, wd, wdt, acts, dcat, hid, acc, sbuf, rbuf,
    sl1, rl1, sr1, rr1, sl2, rl2, sr2, rr2, sz, rz, zsum, mine,
    i_sem, w_sem, zs_sem, zr_sem, rs_sem, rr_sem, as_sem, ar_sem, ds_sem, dr_sem, es_sem, er_sem,
    ps_sem, pr_sem, qs_sem, qr_sem, fs_sem, fr_sem,
):
    dp = lax.axis_index("dp")
    ex = lax.axis_index("expert")
    rem, div = lax.rem, lax.div
    z, xl, y = rem(dp, NZ), rem(div(dp, NZ), 2), div(dp, 2 * NZ)
    xh, c = div(ex, 2), rem(ex, 2)
    x = xh * 2 + xl

    xs = [x] + [rem(x + d, NX) for d in range(1, NX)]
    ys = [y] + [rem(y + d, NY) for d in range(1, NY)]
    zs = [z] + [rem(z + d, NZ) for d in range(1, NZ)]
    xhs, xls = [div(v, 2) for v in xs], [rem(v, 2) for v in xs]
    planes = [[(ys[j] * 2 + xls[i], xhs[i] * 2 + c) for j in range(NY)] for i in range(NX)]
    here = planes[0][0][0] * NZ
    sibling = (dp, ex + 1 - 2 * c)
    along_z = [(here + zs[d], ex) for d in range(NZ)]
    around = {(i, j): (planes[i][j][0] * NZ + z, planes[i][j][1]) for i in range(NX) for j in range(NY) if i * j == 0}

    def at(dx, dy_):
        return around[dx % NX, dy_ % NY]

    def zdev(d):
        return along_z[d % NZ]

    def cell(dx, dy_):
        group, quarter = planes[dx % NX][dy_ % NY]
        return quarter, group

    pairs = ((tok_hbm, tok_ref), (dy_hbm, dy_ref), (ids_hbm, ids_ref), (gw_hbm, gw_ref))
    inputs = [pltpu.make_async_copy(src, dst, i_sem.at[i]) for i, (src, dst) in enumerate(pairs)]
    for copy in inputs:
        copy.start()

    barrier = pltpu.get_barrier_semaphore()
    peers = [zdev(d) for d in PEERS_Z]
    peers += [at(d, 0) for d in range(1, NX)] + [at(0, d) for d in range(1, NY)] + [sibling]
    for peer in peers:
        pl.semaphore_signal(barrier, inc=1, device_id=peer, device_id_type=MESH)

    loads = [pltpu.make_async_copy(wd_hbm.at[0], wd, w_sem.at[2 * NQ])]
    for q in range(NQ):
        for i, ref in enumerate((wg_hbm, wu_hbm)):
            part = ref.at[0, pl.ds(q * QF, QF)]
            loads.append(pltpu.make_async_copy(part, wgu.at[q, :, pl.ds(i * HID, HID)], w_sem.at[2 * q + i]))
    for copy in loads:
        copy.start()

    for copy in inputs:
        copy.wait()

    stage[...] = jnp.zeros_like(stage)
    for i, ref in enumerate((tok_ref, dy_ref)):
        v = ref[...].astype(F32)
        stage[pl.ds(6 * i, TOK), :] = v[:, :HALF]
        stage[pl.ds(6 * i + TOK, TOK), :] = v[:, HALF:]
    lane = lax.broadcasted_iota(jnp.int32, (1, 128), 1)
    for t in range(TOK):
        w = jnp.zeros((1, 128), F32)
        for k in range(2):
            w = w + jnp.where(ids_ref[k, t] == lane % 4, gw_ref[k, t], 0.0)
        hi = w.astype(BF).astype(F32)
        mid = (w - hi).astype(BF).astype(F32)
        low = w - hi - mid
        w = jnp.where(lane < 4, hi, jnp.where(lane < 8, mid, jnp.where(lane < 12, low, 0.0)))
        stage[pl.ds(12 + t, 1), pl.ds(0, 128)] = w
    zb[z] = stage[...].astype(BF)

    pl.semaphore_wait(barrier, len(peers))

    def remote(src, dst, ssem, rsem, device):
        return pltpu.make_async_remote_copy(
            src_ref=src, dst_ref=dst, send_sem=ssem, recv_sem=rsem, device_id=device, device_id_type=MESH
        )

    sends = []

    def send(src, dst, ssem, rsem, device):
        copy = remote(src, dst, ssem, rsem, device)
        copy.start()
        sends.append(copy)

    def pass_on(origin, step, d):
        ref = zb.at[zs[origin % NZ]]
        send(ref, ref, zs_sem.at[d % NZ], zr_sem.at[d % NZ], zdev(step))

    for d in (4, -4, 2, -2, 1, -1):
        pass_on(0, d, d)

    def arrived(d):
        ref = zb.at[zs[-d % NZ]]
        remote(ref, ref, zs_sem.at[d % NZ], zr_sem.at[d % NZ], sibling).wait_recv()

    arrived(4)
    for step in (4, 3, 2, 1, -1):
        pass_on(-4, step, 4 + step)
    arrived(-4)
    for step in (-3, -2, -1, 1):
        pass_on(4, step, step - 4)
    for copy in loads:
        copy.wait()
    for q in range(NQ):
        wgut[q] = wgu[q].T
        wdt[q] = wd[:, pl.ds(q * QF, QF)].T

    for d in (1, -1, 2, -2, 3, -3, 5, -5, 6, -6, 7, -7, 8):
        arrived(d)

    r = lax.broadcasted_iota(jnp.int32, (5 * GROUP, NZ * 16), 0)
    s = lax.broadcasted_iota(jnp.int32, (5 * GROUP, NZ * 16), 1)
    k = s % 16
    kind = (k * 11) // 32
    pick = ((r == kind * GROUP + (s // 16) * TOK + (k - 3 * kind)) & (k < 15)).astype(F32).astype(BF)
    rows = dot(pick, zb[...].reshape(NZ * 16, HALF)).astype(BF)
    mq, mg = cell(0, 0)
    tk[mq, mg, :, pl.ds(0, HALF)] = rows[0:GROUP]
    tk[mq, mg, :, pl.ds(HALF, HALF)] = rows[GROUP : 2 * GROUP]
    dy[mq, mg, :, pl.ds(0, HALF)] = rows[2 * GROUP : 3 * GROUP]
    dy[mq, mg, :, pl.ds(HALF, HALF)] = rows[3 * GROUP : 4 * GROUP]
    rt[mg] = rows[4 * GROUP : 5 * GROUP, 0:128]

    arrays = ((tk, 0), (dy, 1))

    def off(h, first, second):
        return (first, second) if h == 0 else (second, first)

    def block(h, first, second, part=None):
        q_, g_ = cell(*off(h, first, second))
        if part is None:
            return arrays[h][0].at[q_, g_]
        return arrays[h][0].at[q_, g_, :, pl.ds(part * HALF, HALF)]

    def to_sibling(h, first, second, part=None):
        ref = block(h, first, second, part)
        n = (first % 4) * 4 + second % 4
        if part == 1:
            n = 20 if second == 0 else 16 + first % 4
        send(ref, ref, ds_sem.at[h, n], dr_sem.at[h, n], sibling)

    def spot(first, d):
        return (d, 0) if first is None else (first, d)

    def sems(h, first, kind):
        n = 0 if first is None else 1 + first % 4
        return as_sem.at[h, n, kind], ar_sem.at[h, n, kind]

    def to_next(h, first, d, step, kind, part=None):
        ref = block(h, *spot(first, d), part)
        send(ref, ref, *sems(h, first, kind), at(*off(h, *((step, 0) if first is None else (0, step)))))

    def both_ways(h, first):
        to_next(h, first, 0, 1, 0)
        to_next(h, first, 0, -1, 1)

    def wait_near(h, first, kind):
        d = -1 if kind == 0 else 1
        ref = block(h, *spot(first, d))
        remote(ref, ref, *sems(h, first, kind), sibling).wait_recv()
        to_next(h, first, d, -d, 2 + kind, kind)

    def wait_far(h, first):
        for part in range(2):
            ref = block(h, *spot(first, 2), part)
            remote(ref, ref, *sems(h, first, 2 + part), sibling).wait_recv()
            to_sibling(h, *spot(first, 2), part)

    for h in range(2):
        both_ways(h, None)

    def group(dx, dy_):
        return rt.at[planes[dx % NX][dy_ % NY][0]]

    for d in range(1, 4):
        send(group(0, 0), group(0, 0), rs_sem.at[3 + d], rr_sem.at[3 + d], at(0, d))
    for h in range(2):
        both_ways(h, 0)
    for h in range(2):
        to_sibling(h, 0, 0)
    for kind in range(2):
        for h in range(2):
            wait_near(h, None, kind)
            both_ways(h, 2 * kind - 1)
            to_sibling(h, 2 * kind - 1, 0)
    for kind in range(2):
        for h in range(2):
            wait_near(h, 0, kind)
            to_sibling(h, 0, 2 * kind - 1)
    for d in range(4):
        ref = group(0, d)
        if d > 0:
            remote(ref, ref, rs_sem.at[7 - d], rr_sem.at[7 - d], sibling).wait_recv()
        send(ref, ref, rs_sem.at[d], rr_sem.at[d], at(1 if d < 2 else -1, 0))
    for h in range(2):
        wait_far(h, None)
        both_ways(h, 2)
    for first in (-1, 1, 2):
        for kind in range(2):
            for h in range(2):
                wait_near(h, first, kind)
                to_sibling(h, first, 2 * kind - 1)
    for first in (0, -1, 1, 2):
        for h in range(2):
            wait_far(h, first)
    for d in range(4):
        ref = group(1, d)
        remote(ref, ref, rs_sem.at[d], rr_sem.at[d], sibling).wait_recv()
    route = rt[...].reshape(ROWS, 128).astype(F32)
    route_lane = lax.broadcasted_iota(jnp.int32, (ROWS, 128), 1)
    weight = jnp.sum(jnp.where(route_lane % 4 == ex, route, 0.0), axis=1, keepdims=True)

    def forward(q, fresh):
        part = dot(tk[q].reshape(ROWS, QF), wgu[q])
        g[q] = (weight * dy[q].reshape(ROWS, QF).astype(F32)).astype(BF)
        back = dot(g[q], wdt[q])
        if fresh:
            acts[:, pl.ds(0, 2 * HID)] = part
            acts[:, pl.ds(2 * HID, HID)] = back
        else:
            acts[:, pl.ds(0, 2 * HID)] += part
            acts[:, pl.ds(2 * HID, HID)] += back

    forward(c, True)
    forward(2 + c, False)
    for n in range(21):
        for h in range(2):
            first, second = (n // 4, n % 4) if n < 16 else (2, 0) if n == 20 else (n - 16, 2)
            quarter, row = cell(*off(h, first, second))
            ref = arrays[h][0].at[quarter + 1 - 2 * c, row]
            if n < 16 and n % 4 == 2 or n == 8 or n >= 16:
                ref = ref.at[:, pl.ds(HALF if n >= 16 else 0, HALF)]
            remote(ref, ref, ds_sem.at[h, n], dr_sem.at[h, n], sibling).wait_recv()
    forward(1 - c, False)
    forward(3 - c, False)
    gate, up, dh = acts[:, pl.ds(0, HID)], acts[:, pl.ds(HID, HID)], acts[:, pl.ds(2 * HID, HID)]
    sigma = jax.nn.sigmoid(gate)
    active = gate * sigma
    hid[...] = (active * up).astype(BF)
    dcat[:, pl.ds(0, HID)] = (dh * up * (sigma + active * (1.0 - sigma))).astype(BF)
    dcat[:, pl.ds(HID, HID)] = (dh * active).astype(BF)

    sides = ((sl1, rl1, sl2, rl2), (sr1, rr1, sr2, rr2))

    def home(h, first, second):
        px, py = off(h, first, second)
        return xhs[px], planes[px][py][0]

    def both_cores(h, first, second):
        a, b = home(h, first, second)
        cols = pl.ds(h * HALF, HALF)
        return acc[a, b, :, cols] + rbuf[a, b, :, cols].astype(F32)

    def first_axis(h, d, second):
        s1, r1, _, _ = sides[h]
        s1[d, second] = both_cores(h, d, second).astype(BF)
        sem = ps_sem.at[h, d, second], pr_sem.at[h, d, second]
        send(s1.at[d, second], r1.at[d, second], *sem, at(*off(h, d, 0)))

    near, far = xh, 1 - xh

    def piece(ref, i, h):
        return ref.at[(far, near)[i], :, :, pl.ds(h * HALF, HALF)]

    for i, a in enumerate((far, near)):
        sbuf[a] = dot(dcat[...], wgut[2 * a + 1 - c]).astype(BF).reshape(NG, GROUP, QF)
        for h in (1, 0):
            send(piece(sbuf, i, h), piece(rbuf, i, h), es_sem.at[i, h], er_sem.at[i, h], sibling)

    def from_sibling(i, h):
        remote(piece(sbuf, i, h), piece(rbuf, i, h), es_sem.at[i, h], er_sem.at[i, h], sibling).wait_recv()

    acc[far] = dot(dcat[...], wgut[2 * far + c]).reshape(NG, GROUP, QF)
    from_sibling(0, 1)
    for d in (2, 1, 3):
        first_axis(1, d, 2)
    from_sibling(0, 0)
    for second in (2, 1, 3, 0):
        first_axis(0, 2, second)
    acc[near] = dot(dcat[...], wgut[2 * near + c]).reshape(NG, GROUP, QF)
    for h in (1, 0):
        from_sibling(1, h)
    for second in (2, 1, 3, 0):
        for d in (1, 3):
            first_axis(0, d, second)
        if second != 2:
            for d in (2, 1, 3):
                first_axis(1, d, second)

    for second in (2, 1, 3, 0):
        for h in range(2):
            s1, r1, s2, r2 = sides[h]
            total = both_cores(h, 0, second)
            for d in range(1, 4):
                sem = ps_sem.at[h, d, second], pr_sem.at[h, d, second]
                remote(s1.at[d, second], r1.at[d, second], *sem, sibling).wait_recv()
                total = total + r1[d, second].astype(F32)
            if second == 0:
                mine[:, pl.ds(h * HALF, HALF)] = total
            else:
                s2[second] = total.astype(BF)
                send(s2.at[second], r2.at[second], qs_sem.at[h, second], qr_sem.at[h, second], at(*off(h, 0, second)))
    for h in range(2):
        s1, r1, s2, r2 = sides[h]
        total = mine[:, pl.ds(h * HALF, HALF)]
        for d in range(1, 4):
            remote(s2.at[d], r2.at[d], qs_sem.at[h, d], qr_sem.at[h, d], sibling).wait_recv()
            total = total + r2[d].astype(F32)
        zsum[:, pl.ds(h * HALF, HALF)] = total.astype(BF)

    r = lax.broadcasted_iota(jnp.int32, (NZ * 16, GROUP), 0)
    s = lax.broadcasted_iota(jnp.int32, (NZ * 16, GROUP), 1)
    packed = jnp.zeros((NZ * 16, 256), F32)
    for third in range(3):
        k = r % 16 - 3 * third
        place = ((k >= 0) & (k < TOK) & (s == (r // 16) * TOK + k)).astype(F32).astype(BF)
        packed = packed + dot(place, zsum[:, pl.ds(256 * third, 256)])
    sz[...] = packed.astype(BF).reshape(NZ, 16, 256)
    def hand_in(step, d):
        send(sz.at[zs[d % NZ]], rz.at[-d % NZ], fs_sem.at[-d % NZ], fr_sem.at[-d % NZ], zdev(step))

    def handed(d):
        remote(sz.at[z], rz.at[d % NZ], fs_sem.at[d % NZ], fr_sem.at[d % NZ], sibling).wait_recv()
        return rz[d % NZ].astype(F32)

    for far in (8, 7, 6, 5, 3):
        hand_in(4 - far, -far)
    for far in (7, 6, 5, 3):
        hand_in(far - 4, far)
    for d in (1, -1, 2, -2):
        hand_in(d, d)
    for q in range(NQ):
        both = lax.dot_general(
            tk[q].reshape(ROWS, QF), dcat[...], (((0,), (0,)), ((), ())), preferred_element_type=F32
        ).astype(BF)
        gg_ref[0, pl.ds(q * QF, QF), :] = both[:, :HID]
        gu_ref[0, pl.ds(q * QF, QF), :] = both[:, HID:]

    for hub, fars in ((4, (3, 5, 6, 7, 8)), (-4, (-3, -5, -6, -7))):
        ref = sz.at[zs[-hub % NZ]]
        total = ref[...].astype(F32)
        for far in fars:
            total = total + handed(far)
        ref[...] = total.astype(BF)
        hand_in(-hub, -hub)
    hid_t = hid[...].T
    for q in range(NQ):
        gd_ref[0, :, pl.ds(q * QF, QF)] = dot(hid_t, g[q]).astype(BF)

    total = sz[z].astype(F32)
    for d in (1, -1, 2, -2, 4, -4):
        total = total + handed(d)
    stage[:, pl.ds(0, 256)] = total
    for third in range(3):
        gx_ref[:, pl.ds(256 * third, 256)] = stage[pl.ds(3 * third, TOK), pl.ds(0, 256)].astype(BF)

    for copy in sends:
        copy.wait_send()


def settle(*refs):
    copies = [pltpu.make_async_copy(refs[i], refs[4 + i], refs[8].at[i]) for i in range(4)]
    for copy in copies:
        copy.start()
    for copy in copies:
        copy.wait()


def shards(tokens, out_grad, expert_ids, gate_weights, w_gate, w_up, w_down):
    vmem = pl.BlockSpec(memory_space=pltpu.VMEM)
    anywhere = pl.BlockSpec(memory_space=pl.ANY)
    dma = pltpu.SemaphoreType.DMA
    results = pl.pallas_call(
        kernel,
        out_shape=(
            pltpu.VMEM((TOK, QF), BF),
            pltpu.VMEM((1, D, HID), BF),
            pltpu.VMEM((1, D, HID), BF),
            pltpu.VMEM((1, HID, D), BF),
        ),
        in_specs=[anywhere] * 7,
        out_specs=(vmem,) * 4,
        scratch_shapes=[
            pltpu.VMEM((TOK, QF), BF),
            pltpu.VMEM((TOK, QF), BF),
            pltpu.SMEM((2, TOK), jnp.int32),
            pltpu.SMEM((2, TOK), F32),
            pltpu.VMEM((16, HALF), F32),
            pltpu.VMEM((NZ, 16, HALF), BF),
            pltpu.VMEM((NQ, NG, GROUP, QF), BF),
            pltpu.VMEM((NQ, NG, GROUP, QF), BF),
            pltpu.VMEM((NG, GROUP, 128), BF),
            pltpu.VMEM((NQ, ROWS, QF), BF),
            pltpu.VMEM((NQ, QF, 2 * HID), BF),
            pltpu.VMEM((NQ, 2 * HID, QF), BF),
            pltpu.VMEM((HID, D), BF),
            pltpu.VMEM((NQ, QF, HID), BF),
            pltpu.VMEM((ROWS, 3 * HID), F32),
            pltpu.VMEM((ROWS, 2 * HID), BF),
            pltpu.VMEM((ROWS, HID), BF),
            pltpu.VMEM((2, NG, GROUP, QF), F32),
            pltpu.VMEM((2, NG, GROUP, QF), BF),
            pltpu.VMEM((2, NG, GROUP, QF), BF),
            pltpu.VMEM((4, 4, GROUP, HALF), BF),
            pltpu.VMEM((4, 4, GROUP, HALF), BF),
            pltpu.VMEM((4, 4, GROUP, HALF), BF),
            pltpu.VMEM((4, 4, GROUP, HALF), BF),
            pltpu.VMEM((4, GROUP, HALF), BF),
            pltpu.VMEM((4, GROUP, HALF), BF),
            pltpu.VMEM((4, GROUP, HALF), BF),
            pltpu.VMEM((4, GROUP, HALF), BF),
            pltpu.VMEM((NZ, 16, 256), BF),
            pltpu.VMEM((NZ, 16, 256), BF),
            pltpu.VMEM((GROUP, QF), BF),
            pltpu.VMEM((GROUP, QF), F32),
            dma((4,)),
            dma((2 * NQ + 1,)),
            dma((NZ,)), dma((NZ,)),
            dma((7,)), dma((7,)),
            dma((2, 5, 4)), dma((2, 5, 4)),
            dma((2, 21)), dma((2, 21)),
            dma((2, 2)), dma((2, 2)),
            dma((2, 4, 4)), dma((2, 4, 4)),
            dma((2, 4)), dma((2, 4)),
            dma((NZ,)), dma((NZ,)),
        ],
        compiler_params=pltpu.CompilerParams(
            collective_id=0, has_side_effects=True, vmem_limit_bytes=56 * 2**20
        ),
        cost_estimate=pl.CostEstimate(flops=2_400_000_000, bytes_accessed=4_800_000, transcendentals=49152),
        name="moe_backward",
    )(tokens, out_grad, expert_ids.T, gate_weights.T, w_gate, w_up, w_down)
    return pl.pallas_call(
        settle,
        out_shape=[jax.ShapeDtypeStruct(v.shape, v.dtype) for v in results],
        in_specs=[anywhere] * 4,
        out_specs=[anywhere] * 4,
        scratch_shapes=[dma((4,))],
        compiler_params=pltpu.CompilerParams(vmem_limit_bytes=2**20),
        name="settle",
    )(*results)


def solution(mesh):
    placed = (
        P("dp", "expert"),
        P("dp", "expert"),
        P("dp", None),
        P("dp", None),
        P("expert", None, "dp"),
        P("expert", None, "dp"),
        P("expert", "dp", None),
    )
    return jax.shard_map(
        shards,
        mesh=mesh,
        in_specs=placed,
        out_specs=(
            P("dp", "expert"),
            P("expert", None, "dp"),
            P("expert", None, "dp"),
            P("expert", "dp", None),
        ),
        check_vma=False,
    )
```

```python
import jax
import jax.numpy as jnp
from jax import lax
from jax.experimental import pallas as pl
from jax.experimental.pallas import tpu as pltpu
from jax.sharding import PartitionSpec as P

MESH = pl.DeviceIdType.MESH
NX, NY, NZ = 4, 4, 16
PEERS_Z = (4, -4, 3, -3, 2, -2, 1, -1)
TOK = 3
QF = 768
NQ = 4
HALF = QF // 2
GROUP = NZ * TOK
NG = 8
ROWS = NG * GROUP
HID = 128
D = NQ * QF
BF, F32 = jnp.bfloat16, jnp.float32


def dot(a, b):
    return jnp.dot(a, b, preferred_element_type=F32)


def kernel(
    tok_hbm, dy_hbm, ids_hbm, gw_hbm, wg_hbm, wu_hbm, wd_hbm,
    gx_ref, gg_ref, gu_ref, gd_ref,
    tok_ref, dy_ref, ids_ref, gw_ref, stage, zb, tk, dy, rt, g, wgu, wgut, wd, wdt, acts, dcat, hid, acc, sbuf, rbuf,
    sl1, rl1, sr1, rr1, sl2, rl2, sr2, rr2, sz, rz, zsum, mine,
    i_sem, w_sem, zs_sem, zr_sem, rs_sem, rr_sem, as_sem, ar_sem, ds_sem, dr_sem, es_sem, er_sem,
    ps_sem, pr_sem, qs_sem, qr_sem, fs_sem, fr_sem,
):
    dp = lax.axis_index("dp")
    ex = lax.axis_index("expert")
    rem, div = lax.rem, lax.div
    z, xl, y = rem(dp, NZ), rem(div(dp, NZ), 2), div(dp, 2 * NZ)
    xh, c = div(ex, 2), rem(ex, 2)
    x = xh * 2 + xl

    xs = [x] + [rem(x + d, NX) for d in range(1, NX)]
    ys = [y] + [rem(y + d, NY) for d in range(1, NY)]
    zs = [z] + [rem(z + NZ + (1 - 2 * c) * d, NZ) for d in range(1, NZ)]
    xhs, xls = [div(v, 2) for v in xs], [rem(v, 2) for v in xs]
    planes = [[(ys[j] * 2 + xls[i], xhs[i] * 2 + c) for j in range(NY)] for i in range(NX)]
    here = planes[0][0][0] * NZ
    sibling = (dp, ex + 1 - 2 * c)
    along_z = [(here + zs[d], ex) for d in range(NZ)]
    around = {(i, j): (planes[i][j][0] * NZ + z, planes[i][j][1]) for i in range(NX) for j in range(NY) if i * j == 0}

    def at(dx, dy_):
        return around[dx % NX, dy_ % NY]

    def zdev(d):
        return along_z[d % NZ]

    def cell(dx, dy_):
        group, quarter = planes[dx % NX][dy_ % NY]
        return quarter, group

    pairs = ((tok_hbm, tok_ref), (dy_hbm, dy_ref), (ids_hbm, ids_ref), (gw_hbm, gw_ref))
    inputs = [pltpu.make_async_copy(src, dst, i_sem.at[i]) for i, (src, dst) in enumerate(pairs)]
    for copy in inputs:
        copy.start()

    barrier = pltpu.get_barrier_semaphore()
    peers = [zdev(d) for d in PEERS_Z]
    peers += [at(d, 0) for d in range(1, NX)] + [at(0, d) for d in range(1, NY)] + [sibling]
    for peer in peers:
        pl.semaphore_signal(barrier, inc=1, device_id=peer, device_id_type=MESH)

    loads = [pltpu.make_async_copy(wd_hbm.at[0], wd, w_sem.at[2 * NQ])]
    for q in range(NQ):
        for i, ref in enumerate((wg_hbm, wu_hbm)):
            part = ref.at[0, pl.ds(q * QF, QF)]
            loads.append(pltpu.make_async_copy(part, wgu.at[q, :, pl.ds(i * HID, HID)], w_sem.at[2 * q + i]))
    for copy in loads:
        copy.start()

    for copy in inputs:
        copy.wait()

    stage[...] = jnp.zeros_like(stage)
    for i, ref in enumerate((tok_ref, dy_ref)):
        v = ref[...].astype(F32)
        stage[pl.ds(6 * i, TOK), :] = v[:, :HALF]
        stage[pl.ds(6 * i + TOK, TOK), :] = v[:, HALF:]
    lane = lax.broadcasted_iota(jnp.int32, (1, 128), 1)
    for t in range(TOK):
        w = jnp.zeros((1, 128), F32)
        for k in range(2):
            w = w + jnp.where(ids_ref[k, t] == lane % 4, gw_ref[k, t], 0.0)
        hi = w.astype(BF).astype(F32)
        mid = (w - hi).astype(BF).astype(F32)
        low = w - hi - mid
        w = jnp.where(lane < 4, hi, jnp.where(lane < 8, mid, jnp.where(lane < 12, low, 0.0)))
        stage[pl.ds(12 + t, 1), pl.ds(0, 128)] = w
    zb[z] = stage[...].astype(BF)

    pl.semaphore_wait(barrier, len(peers))

    def remote(src, dst, ssem, rsem, device):
        return pltpu.make_async_remote_copy(
            src_ref=src, dst_ref=dst, send_sem=ssem, recv_sem=rsem, device_id=device, device_id_type=MESH
        )

    sends = []

    def send(src, dst, ssem, rsem, device):
        copy = remote(src, dst, ssem, rsem, device)
        copy.start()
        sends.append(copy)

    def pass_on(origin, step, d):
        ref = zb.at[zs[origin % NZ]]
        send(ref, ref, zs_sem.at[d % NZ], zr_sem.at[d % NZ], zdev(step))

    for d in (4, -4, 3, -3, 2, -2, 1, -1):
        pass_on(0, d, d)

    def arrived(d):
        ref = zb.at[zs[-d % NZ]]
        remote(ref, ref, zs_sem.at[d % NZ], zr_sem.at[d % NZ], sibling).wait_recv()

    arrived(4)
    for step in (4, 3, 2, 1):
        pass_on(-4, step, 4 + step)
    arrived(-4)
    for step in (-3, -2, -1):
        pass_on(4, step, step - 4)
    for copy in loads:
        copy.wait()
    for q in range(NQ):
        wgut[q] = wgu[q].T
        wdt[q] = wd[:, pl.ds(q * QF, QF)].T

    for d in (1, -1, 2, -2, 3, -3, 5, -5, 6, -6, 7, -7, 8):
        arrived(d)

    r = lax.broadcasted_iota(jnp.int32, (5 * GROUP, NZ * 16), 0)
    s = lax.broadcasted_iota(jnp.int32, (5 * GROUP, NZ * 16), 1)
    k = s % 16
    kind = (k * 11) // 32
    pick = ((r == kind * GROUP + (s // 16) * TOK + (k - 3 * kind)) & (k < 15)).astype(F32).astype(BF)
    rows = dot(pick, zb[...].reshape(NZ * 16, HALF)).astype(BF)
    mq, mg = cell(0, 0)
    tk[mq, mg, :, pl.ds(0, HALF)] = rows[0:GROUP]
    tk[mq, mg, :, pl.ds(HALF, HALF)] = rows[GROUP : 2 * GROUP]
    dy[mq, mg, :, pl.ds(0, HALF)] = rows[2 * GROUP : 3 * GROUP]
    dy[mq, mg, :, pl.ds(HALF, HALF)] = rows[3 * GROUP : 4 * GROUP]
    rt[mg] = rows[4 * GROUP : 5 * GROUP, 0:128]

    arrays = ((tk, 0), (dy, 1))

    def off(h, first, second):
        return (first, second) if h == 0 else (second, first)

    def block(h, first, second, part=None):
        q_, g_ = cell(*off(h, first, second))
        if part is None:
            return arrays[h][0].at[q_, g_]
        return arrays[h][0].at[q_, g_, :, pl.ds(part * HALF, HALF)]

    def to_sibling(h, first, second, part=None):
        ref = block(h, first, second, part)
        n = (first % 4) * 4 + second % 4
        if part == 1:
            n = 20 if second == 0 else 16 + first % 4
        send(ref, ref, ds_sem.at[h, n], dr_sem.at[h, n], sibling)

    def spot(first, d):
        return (d, 0) if first is None else (first, d)

    def sems(h, first, kind):
        n = 0 if first is None else 1 + first % 4
        return as_sem.at[h, n, kind], ar_sem.at[h, n, kind]

    def to_next(h, first, d, step, kind, part=None):
        ref = block(h, *spot(first, d), part)
        send(ref, ref, *sems(h, first, kind), at(*off(h, *((step, 0) if first is None else (0, step)))))

    def both_ways(h, first):
        to_next(h, first, 0, 1, 0)
        to_next(h, first, 0, -1, 1)

    def wait_near(h, first, kind):
        d = -1 if kind == 0 else 1
        ref = block(h, *spot(first, d))
        remote(ref, ref, *sems(h, first, kind), sibling).wait_recv()
        to_next(h, first, d, -d, 2 + kind, kind)

    def wait_far(h, first):
        for part in range(2):
            ref = block(h, *spot(first, 2), part)
            remote(ref, ref, *sems(h, first, 2 + part), sibling).wait_recv()
            to_sibling(h, *spot(first, 2), part)

    for h in range(2):
        both_ways(h, None)

    def group(dx, dy_):
        return rt.at[planes[dx % NX][dy_ % NY][0]]

    for d in range(1, 4):
        send(group(0, 0), group(0, 0), rs_sem.at[3 + d], rr_sem.at[3 + d], at(0, d))
    for h in range(2):
        both_ways(h, 0)
    for h in range(2):
        to_sibling(h, 0, 0)
    for kind in range(2):
        for h in range(2):
            wait_near(h, None, kind)
            both_ways(h, 2 * kind - 1)
            to_sibling(h, 2 * kind - 1, 0)
    for kind in range(2):
        for h in range(2):
            wait_near(h, 0, kind)
            to_sibling(h, 0, 2 * kind - 1)
    for d in range(4):
        ref = group(0, d)
        if d > 0:
            remote(ref, ref, rs_sem.at[7 - d], rr_sem.at[7 - d], sibling).wait_recv()
        send(ref, ref, rs_sem.at[d], rr_sem.at[d], at(1 if d < 2 else -1, 0))
    for h in range(2):
        wait_far(h, None)
        both_ways(h, 2)
    for first in (-1, 1, 2):
        for kind in range(2):
            for h in range(2):
                wait_near(h, first, kind)
                to_sibling(h, first, 2 * kind - 1)
    for first in (0, -1, 1, 2):
        for h in range(2):
            wait_far(h, first)
    for d in range(4):
        ref = group(1, d)
        remote(ref, ref, rs_sem.at[d], rr_sem.at[d], sibling).wait_recv()
    route = rt[...].reshape(ROWS, 128).astype(F32)
    route_lane = lax.broadcasted_iota(jnp.int32, (ROWS, 128), 1)
    weight = jnp.sum(jnp.where(route_lane % 4 == ex, route, 0.0), axis=1, keepdims=True)

    def forward(q, fresh):
        part = dot(tk[q].reshape(ROWS, QF), wgu[q])
        g[q] = (weight * dy[q].reshape(ROWS, QF).astype(F32)).astype(BF)
        back = dot(g[q], wdt[q])
        if fresh:
            acts[:, pl.ds(0, 2 * HID)] = part
            acts[:, pl.ds(2 * HID, HID)] = back
        else:
            acts[:, pl.ds(0, 2 * HID)] += part
            acts[:, pl.ds(2 * HID, HID)] += back

    forward(c, True)
    forward(2 + c, False)
    def from_other_core(side, pair, j):
        dx = ((0, 1 + 2 * xl), (2, 3 - 2 * xl))[side][pair]
        quarter = 2 * (xh, 1 - xh)[side] + 1 - c
        row = ys[j] * 2 + (xl, 1 - xl)[pair]
        for h in range(2):
            ref = arrays[h][0].at[quarter, row]
            n = dx * 4 + j if h == 0 else j * 4 + dx
            opposite_x, same_x = side == 1 and pair == 0, side == 0 and pair == 0
            second_half = None
            if h == 0:
                second_half = 16 + dx if j == 2 else 20 if opposite_x and j == 0 else None
            else:
                second_half = 16 + j if opposite_x else 20 if same_x and j == 2 else None
            pieces = [(n, ref)]
            if second_half is not None:
                pieces = [(n, ref.at[:, pl.ds(0, HALF)]), (second_half, ref.at[:, pl.ds(HALF, HALF)])]
            for m, part in pieces:
                remote(part, part, ds_sem.at[h, m], dr_sem.at[h, m], sibling).wait_recv()

    for side in range(2):
        for pair in range(2):
            for j in range(4):
                from_other_core(side, pair, j)
        forward(2 * (xh, 1 - xh)[side] + 1 - c, False)
    gate, up, dh = acts[:, pl.ds(0, HID)], acts[:, pl.ds(HID, HID)], acts[:, pl.ds(2 * HID, HID)]
    sigma = jax.nn.sigmoid(gate)
    active = gate * sigma
    hid[...] = (active * up).astype(BF)
    dcat[:, pl.ds(0, HID)] = (dh * up * (sigma + active * (1.0 - sigma))).astype(BF)
    dcat[:, pl.ds(HID, HID)] = (dh * active).astype(BF)

    sides = ((sl1, rl1, sl2, rl2), (sr1, rr1, sr2, rr2))

    def home(h, first, second):
        px, py = off(h, first, second)
        return xhs[px], planes[px][py][0]

    def both_cores(h, first, second):
        a, b = home(h, first, second)
        cols = pl.ds(h * HALF, HALF)
        return acc[a, b, :, cols] + rbuf[a, b, :, cols].astype(F32)

    def first_axis(h, d, second):
        s1, r1, _, _ = sides[h]
        s1[d, second] = both_cores(h, d, second).astype(BF)
        sem = ps_sem.at[h, d, second], pr_sem.at[h, d, second]
        send(s1.at[d, second], r1.at[d, second], *sem, at(*off(h, d, 0)))

    near, far = xh, 1 - xh

    def piece(ref, i, h):
        return ref.at[(far, near)[i], :, :, pl.ds(h * HALF, HALF)]

    for i, a in enumerate((far, near)):
        for h in (1, 0):
            cols = pl.ds(h * HALF, HALF)
            sbuf[a, :, :, cols] = dot(dcat[...], wgut[2 * a + 1 - c, :, cols]).astype(BF).reshape(NG, GROUP, HALF)
            send(piece(sbuf, i, h), piece(rbuf, i, h), es_sem.at[i, h], er_sem.at[i, h], sibling)

    def from_sibling(i, h):
        remote(piece(sbuf, i, h), piece(rbuf, i, h), es_sem.at[i, h], er_sem.at[i, h], sibling).wait_recv()

    acc[far] = dot(dcat[...], wgut[2 * far + c]).reshape(NG, GROUP, QF)
    from_sibling(0, 1)
    for d in (2, 1, 3):
        first_axis(1, d, 2)
    from_sibling(0, 0)
    for second in (2, 1, 3, 0):
        first_axis(0, 2, second)
    acc[near] = dot(dcat[...], wgut[2 * near + c]).reshape(NG, GROUP, QF)
    for h in (1, 0):
        from_sibling(1, h)
    for second in (2, 1, 3, 0):
        for d in (1, 3):
            first_axis(0, d, second)
        if second != 2:
            for d in (2, 1, 3):
                first_axis(1, d, second)

    for second in (2, 1, 3, 0):
        for h in range(2):
            s1, r1, s2, r2 = sides[h]
            total = both_cores(h, 0, second)
            for d in range(1, 4):
                sem = ps_sem.at[h, d, second], pr_sem.at[h, d, second]
                remote(s1.at[d, second], r1.at[d, second], *sem, sibling).wait_recv()
                total = total + r1[d, second].astype(F32)
            if second == 0:
                mine[:, pl.ds(h * HALF, HALF)] = total
            else:
                s2[second] = total.astype(BF)
                send(s2.at[second], r2.at[second], qs_sem.at[h, second], qr_sem.at[h, second], at(*off(h, 0, second)))
    for h in range(2):
        s1, r1, s2, r2 = sides[h]
        total = mine[:, pl.ds(h * HALF, HALF)]
        for d in range(1, 4):
            remote(s2.at[d], r2.at[d], qs_sem.at[h, d], qr_sem.at[h, d], sibling).wait_recv()
            total = total + r2[d].astype(F32)
        zsum[:, pl.ds(h * HALF, HALF)] = total.astype(BF)

    r = lax.broadcasted_iota(jnp.int32, (NZ * 16, GROUP), 0)
    s = lax.broadcasted_iota(jnp.int32, (NZ * 16, GROUP), 1)
    packed = jnp.zeros((NZ * 16, 256), F32)
    for third in range(3):
        k = r % 16 - 3 * third
        place = ((k >= 0) & (k < TOK) & (s == (r // 16) * TOK + k)).astype(F32).astype(BF)
        packed = packed + dot(place, zsum[:, pl.ds(256 * third, 256)])
    sz[...] = packed.astype(BF).reshape(NZ, 16, 256)
    def hand_in(step, d):
        send(sz.at[zs[d % NZ]], rz.at[-d % NZ], fs_sem.at[-d % NZ], fr_sem.at[-d % NZ], zdev(step))

    def handed(d):
        remote(sz.at[z], rz.at[d % NZ], fs_sem.at[d % NZ], fr_sem.at[d % NZ], sibling).wait_recv()
        return rz[d % NZ].astype(F32)

    for away in (8, 7, 6, 5):
        hand_in(4 - away, -away)
    for away in (7, 6, 5):
        hand_in(away - 4, away)
    for d in (3, -3, 2, -2, 1, -1):
        hand_in(d, d)
    for q in range(NQ):
        both = lax.dot_general(
            tk[q].reshape(ROWS, QF), dcat[...], (((0,), (0,)), ((), ())), preferred_element_type=F32
        ).astype(BF)
        gg_ref[0, pl.ds(q * QF, QF), :] = both[:, :HID]
        gu_ref[0, pl.ds(q * QF, QF), :] = both[:, HID:]

    for hub, fars in ((4, (5, 6, 7, 8)), (-4, (-5, -6, -7))):
        ref = sz.at[zs[-hub % NZ]]
        total = ref[...].astype(F32)
        for far in fars:
            total = total + handed(far)
        ref[...] = total.astype(BF)
        hand_in(-hub, -hub)
    hid_t = hid[...].T
    for q in range(NQ):
        gd_ref[0, :, pl.ds(q * QF, QF)] = dot(hid_t, g[q]).astype(BF)

    total = sz[z].astype(F32)
    for d in (1, -1, 2, -2, 3, -3, 4, -4):
        total = total + handed(d)
    stage[:, pl.ds(0, 256)] = total
    for third in range(3):
        gx_ref[:, pl.ds(256 * third, 256)] = stage[pl.ds(3 * third, TOK), pl.ds(0, 256)].astype(BF)

    for copy in sends:
        copy.wait_send()


def settle(*refs):
    copies = [pltpu.make_async_copy(refs[i], refs[4 + i], refs[8].at[i]) for i in range(4)]
    for copy in copies:
        copy.start()
    for copy in copies:
        copy.wait()


def shards(tokens, out_grad, expert_ids, gate_weights, w_gate, w_up, w_down):
    vmem = pl.BlockSpec(memory_space=pltpu.VMEM)
    anywhere = pl.BlockSpec(memory_space=pl.ANY)
    dma = pltpu.SemaphoreType.DMA
    results = pl.pallas_call(
        kernel,
        out_shape=(
            pltpu.VMEM((TOK, QF), BF),
            pltpu.VMEM((1, D, HID), BF),
            pltpu.VMEM((1, D, HID), BF),
            pltpu.VMEM((1, HID, D), BF),
        ),
        in_specs=[anywhere] * 7,
        out_specs=(vmem,) * 4,
        scratch_shapes=[
            pltpu.VMEM((TOK, QF), BF),
            pltpu.VMEM((TOK, QF), BF),
            pltpu.SMEM((2, TOK), jnp.int32),
            pltpu.SMEM((2, TOK), F32),
            pltpu.VMEM((16, HALF), F32),
            pltpu.VMEM((NZ, 16, HALF), BF),
            pltpu.VMEM((NQ, NG, GROUP, QF), BF),
            pltpu.VMEM((NQ, NG, GROUP, QF), BF),
            pltpu.VMEM((NG, GROUP, 128), BF),
            pltpu.VMEM((NQ, ROWS, QF), BF),
            pltpu.VMEM((NQ, QF, 2 * HID), BF),
            pltpu.VMEM((NQ, 2 * HID, QF), BF),
            pltpu.VMEM((HID, D), BF),
            pltpu.VMEM((NQ, QF, HID), BF),
            pltpu.VMEM((ROWS, 3 * HID), F32),
            pltpu.VMEM((ROWS, 2 * HID), BF),
            pltpu.VMEM((ROWS, HID), BF),
            pltpu.VMEM((2, NG, GROUP, QF), F32),
            pltpu.VMEM((2, NG, GROUP, QF), BF),
            pltpu.VMEM((2, NG, GROUP, QF), BF),
            pltpu.VMEM((4, 4, GROUP, HALF), BF),
            pltpu.VMEM((4, 4, GROUP, HALF), BF),
            pltpu.VMEM((4, 4, GROUP, HALF), BF),
            pltpu.VMEM((4, 4, GROUP, HALF), BF),
            pltpu.VMEM((4, GROUP, HALF), BF),
            pltpu.VMEM((4, GROUP, HALF), BF),
            pltpu.VMEM((4, GROUP, HALF), BF),
            pltpu.VMEM((4, GROUP, HALF), BF),
            pltpu.VMEM((NZ, 16, 256), BF),
            pltpu.VMEM((NZ, 16, 256), BF),
            pltpu.VMEM((GROUP, QF), BF),
            pltpu.VMEM((GROUP, QF), F32),
            dma((4,)),
            dma((2 * NQ + 1,)),
            dma((NZ,)), dma((NZ,)),
            dma((7,)), dma((7,)),
            dma((2, 5, 4)), dma((2, 5, 4)),
            dma((2, 21)), dma((2, 21)),
            dma((2, 2)), dma((2, 2)),
            dma((2, 4, 4)), dma((2, 4, 4)),
            dma((2, 4)), dma((2, 4)),
            dma((NZ,)), dma((NZ,)),
        ],
        compiler_params=pltpu.CompilerParams(
            collective_id=0, has_side_effects=True, vmem_limit_bytes=56 * 2**20
        ),
        cost_estimate=pl.CostEstimate(flops=2_400_000_000, bytes_accessed=4_800_000, transcendentals=49152),
        name="moe_backward",
    )(tokens, out_grad, expert_ids.T, gate_weights.T, w_gate, w_up, w_down)
    return pl.pallas_call(
        settle,
        out_shape=[jax.ShapeDtypeStruct(v.shape, v.dtype) for v in results],
        in_specs=[anywhere] * 4,
        out_specs=[anywhere] * 4,
        scratch_shapes=[dma((4,))],
        compiler_params=pltpu.CompilerParams(vmem_limit_bytes=2**20),
        name="settle",
    )(*results)


def solution(mesh):
    placed = (
        P("dp", "expert"),
        P("dp", "expert"),
        P("dp", None),
        P("dp", None),
        P("expert", None, "dp"),
        P("expert", None, "dp"),
        P("expert", "dp", None),
    )
    return jax.shard_map(
        shards,
        mesh=mesh,
        in_specs=placed,
        out_specs=(
            P("dp", "expert"),
            P("expert", None, "dp"),
            P("expert", None, "dp"),
            P("expert", "dp", None),
        ),
        check_vma=False,
    )
```

```python
import jax
import jax.numpy as jnp
from jax import lax
from jax.experimental import pallas as pl
from jax.experimental.pallas import tpu as pltpu
from jax.sharding import PartitionSpec as P

MESH = pl.DeviceIdType.MESH
NX, NY, NZ = 4, 4, 16
PEERS_Z = (4, -4, 3, -3, 2, -2, 1, -1)
TOK = 3
QF = 768
NQ = 4
HALF = QF // 2
GROUP = NZ * TOK
NG = 8
ROWS = NG * GROUP
HID = 128
D = NQ * QF
BF, F32 = jnp.bfloat16, jnp.float32


def dot(a, b):
    return jnp.dot(a, b, preferred_element_type=F32)


def kernel(
    tok_hbm, dy_hbm, ids_hbm, gw_hbm, wg_hbm, wu_hbm, wd_hbm,
    gx_ref, gg_ref, gu_ref, gd_ref,
    tok_ref, dy_ref, ids_ref, gw_ref, stage, zb, tk, dy, rt, g, wgu, wgut, wd, wdt, acts, dcat, hid, acc, sbuf, rbuf,
    sl1, rl1, sr1, rr1, sl2, rl2, sr2, rr2, sz, rz, zsum, mine,
    i_sem, w_sem, zs_sem, zr_sem, rs_sem, rr_sem, as_sem, ar_sem, ds_sem, dr_sem, es_sem, er_sem,
    ps_sem, pr_sem, qs_sem, qr_sem, fs_sem, fr_sem,
):
    dp = lax.axis_index("dp")
    ex = lax.axis_index("expert")
    rem, div = lax.rem, lax.div
    z, xl, y = rem(dp, NZ), rem(div(dp, NZ), 2), div(dp, 2 * NZ)
    xh, c = div(ex, 2), rem(ex, 2)
    x = xh * 2 + xl

    xs = [x] + [rem(x + d, NX) for d in range(1, NX)]
    ys = [y] + [rem(y + d, NY) for d in range(1, NY)]
    zs = [z] + [rem(z + NZ + (1 - 2 * c) * d, NZ) for d in range(1, NZ)]
    xhs, xls = [div(v, 2) for v in xs], [rem(v, 2) for v in xs]
    planes = [[(ys[j] * 2 + xls[i], xhs[i] * 2 + c) for j in range(NY)] for i in range(NX)]
    here = planes[0][0][0] * NZ
    sibling = (dp, ex + 1 - 2 * c)
    along_z = [(here + zs[d], ex) for d in range(NZ)]
    around = {(i, j): (planes[i][j][0] * NZ + z, planes[i][j][1]) for i in range(NX) for j in range(NY) if i * j == 0}

    def at(dx, dy_):
        return around[dx % NX, dy_ % NY]

    def zdev(d):
        return along_z[d % NZ]

    def cell(dx, dy_):
        group, quarter = planes[dx % NX][dy_ % NY]
        return quarter, group

    pairs = ((tok_hbm, tok_ref), (dy_hbm, dy_ref), (ids_hbm, ids_ref), (gw_hbm, gw_ref))
    inputs = [pltpu.make_async_copy(src, dst, i_sem.at[i]) for i, (src, dst) in enumerate(pairs)]
    for copy in inputs:
        copy.start()

    barrier = pltpu.get_barrier_semaphore()
    peers = [zdev(d) for d in PEERS_Z]
    peers += [at(d, 0) for d in range(1, NX)] + [at(0, d) for d in range(1, NY)] + [sibling]
    for peer in peers:
        pl.semaphore_signal(barrier, inc=1, device_id=peer, device_id_type=MESH)

    for copy in inputs:
        copy.wait()

    stage[...] = jnp.zeros_like(stage)
    for i, ref in enumerate((tok_ref, dy_ref)):
        v = ref[...].astype(F32)
        stage[pl.ds(6 * i, TOK), :] = v[:, :HALF]
        stage[pl.ds(6 * i + TOK, TOK), :] = v[:, HALF:]
    lane = lax.broadcasted_iota(jnp.int32, (1, 128), 1)
    for t in range(TOK):
        w = jnp.zeros((1, 128), F32)
        for k in range(2):
            w = w + jnp.where(ids_ref[k, t] == lane % 4, gw_ref[k, t], 0.0)
        hi = w.astype(BF).astype(F32)
        mid = (w - hi).astype(BF).astype(F32)
        low = w - hi - mid
        w = jnp.where(lane < 4, hi, jnp.where(lane < 8, mid, jnp.where(lane < 12, low, 0.0)))
        stage[pl.ds(12 + t, 1), pl.ds(0, 128)] = w
    zb[z] = stage[...].astype(BF)

    pl.semaphore_wait(barrier, len(peers))

    def remote(src, dst, ssem, rsem, device):
        return pltpu.make_async_remote_copy(
            src_ref=src, dst_ref=dst, send_sem=ssem, recv_sem=rsem, device_id=device, device_id_type=MESH
        )

    sends = []

    def send(src, dst, ssem, rsem, device):
        copy = remote(src, dst, ssem, rsem, device)
        copy.start()
        sends.append(copy)

    def pass_on(origin, step, d):
        ref = zb.at[zs[origin % NZ]]
        send(ref, ref, zs_sem.at[d % NZ], zr_sem.at[d % NZ], zdev(step))

    for d in (4, -4, 3, -3, 2, -2, 1, -1):
        pass_on(0, d, d)

    loads = [pltpu.make_async_copy(wd_hbm.at[0], wd, w_sem.at[2 * NQ])]
    for q in range(NQ):
        for i, ref in enumerate((wg_hbm, wu_hbm)):
            part = ref.at[0, pl.ds(q * QF, QF)]
            loads.append(pltpu.make_async_copy(part, wgu.at[q, :, pl.ds(i * HID, HID)], w_sem.at[2 * q + i]))
    for copy in loads:
        copy.start()

    def arrived(d):
        ref = zb.at[zs[-d % NZ]]
        remote(ref, ref, zs_sem.at[d % NZ], zr_sem.at[d % NZ], sibling).wait_recv()

    arrived(4)
    for step in (4, 3, 2, 1):
        pass_on(-4, step, 4 + step)
    arrived(-4)
    for step in (-3, -2, -1):
        pass_on(4, step, step - 4)
    for copy in loads:
        copy.wait()
    for q in range(NQ):
        wgut[q] = wgu[q].T
        wdt[q] = wd[:, pl.ds(q * QF, QF)].T

    for d in (1, -1, 2, -2, 3, -3, 5, -5, 6, -6, 7, -7, 8):
        arrived(d)

    r = lax.broadcasted_iota(jnp.int32, (5 * GROUP, NZ * 16), 0)
    s = lax.broadcasted_iota(jnp.int32, (5 * GROUP, NZ * 16), 1)
    k = s % 16
    kind = (k * 11) // 32
    pick = ((r == kind * GROUP + (s // 16) * TOK + (k - 3 * kind)) & (k < 15)).astype(F32).astype(BF)
    rows = dot(pick, zb[...].reshape(NZ * 16, HALF)).astype(BF)
    mq, mg = cell(0, 0)
    tk[mq, mg, :, pl.ds(0, HALF)] = rows[0:GROUP]
    tk[mq, mg, :, pl.ds(HALF, HALF)] = rows[GROUP : 2 * GROUP]
    dy[mq, mg, :, pl.ds(0, HALF)] = rows[2 * GROUP : 3 * GROUP]
    dy[mq, mg, :, pl.ds(HALF, HALF)] = rows[3 * GROUP : 4 * GROUP]
    rt[mg] = rows[4 * GROUP : 5 * GROUP, 0:128]

    arrays = ((tk, 0), (dy, 1))

    def off(h, first, second):
        return (first, second) if h == 0 else (second, first)

    def block(h, first, second, part=None):
        q_, g_ = cell(*off(h, first, second))
        if part is None:
            return arrays[h][0].at[q_, g_]
        return arrays[h][0].at[q_, g_, :, pl.ds(part * HALF, HALF)]

    def to_sibling(h, first, second, part=None):
        ref = block(h, first, second, part)
        n = (first % 4) * 4 + second % 4
        if part == 1:
            n = 20 if second == 0 else 16 + first % 4
        send(ref, ref, ds_sem.at[h, n], dr_sem.at[h, n], sibling)

    def spot(first, d):
        return (d, 0) if first is None else (first, d)

    def sems(h, first, kind):
        n = 0 if first is None else 1 + first % 4
        return as_sem.at[h, n, kind], ar_sem.at[h, n, kind]

    def to_next(h, first, d, step, kind, part=None):
        ref = block(h, *spot(first, d), part)
        send(ref, ref, *sems(h, first, kind), at(*off(h, *((step, 0) if first is None else (0, step)))))

    def both_ways(h, first):
        to_next(h, first, 0, 1, 0)
        to_next(h, first, 0, -1, 1)

    def wait_near(h, first, kind):
        d = -1 if kind == 0 else 1
        ref = block(h, *spot(first, d))
        remote(ref, ref, *sems(h, first, kind), sibling).wait_recv()
        to_next(h, first, d, -d, 2 + kind, kind)

    def wait_far(h, first):
        for part in range(2):
            ref = block(h, *spot(first, 2), part)
            remote(ref, ref, *sems(h, first, 2 + part), sibling).wait_recv()
            to_sibling(h, *spot(first, 2), part)

    for h in range(2):
        both_ways(h, None)

    def group(dx, dy_):
        return rt.at[planes[dx % NX][dy_ % NY][0]]

    for d in range(1, 4):
        send(group(0, 0), group(0, 0), rs_sem.at[3 + d], rr_sem.at[3 + d], at(0, d))
    for h in range(2):
        both_ways(h, 0)
    for h in range(2):
        to_sibling(h, 0, 0)
    for kind in range(2):
        for h in range(2):
            wait_near(h, None, kind)
            both_ways(h, 2 * kind - 1)
            to_sibling(h, 2 * kind - 1, 0)
    for kind in range(2):
        for h in range(2):
            wait_near(h, 0, kind)
            to_sibling(h, 0, 2 * kind - 1)
    for d in range(4):
        ref = group(0, d)
        if d > 0:
            remote(ref, ref, rs_sem.at[7 - d], rr_sem.at[7 - d], sibling).wait_recv()
        send(ref, ref, rs_sem.at[d], rr_sem.at[d], at(1 if d < 2 else -1, 0))
    for h in range(2):
        wait_far(h, None)
        both_ways(h, 2)
    for first in (-1, 1, 2):
        for kind in range(2):
            for h in range(2):
                wait_near(h, first, kind)
                to_sibling(h, first, 2 * kind - 1)
    for first in (0, -1, 1, 2):
        for h in range(2):
            wait_far(h, first)
    for d in range(4):
        ref = group(1, d)
        remote(ref, ref, rs_sem.at[d], rr_sem.at[d], sibling).wait_recv()
    route = rt[...].reshape(ROWS, 128).astype(F32)
    route_lane = lax.broadcasted_iota(jnp.int32, (ROWS, 128), 1)
    weight = jnp.sum(jnp.where(route_lane % 4 == ex, route, 0.0), axis=1, keepdims=True)

    def forward(q, fresh):
        part = dot(tk[q].reshape(ROWS, QF), wgu[q])
        g[q] = (weight * dy[q].reshape(ROWS, QF).astype(F32)).astype(BF)
        back = dot(g[q], wdt[q])
        if fresh:
            acts[:, pl.ds(0, 2 * HID)] = part
            acts[:, pl.ds(2 * HID, HID)] = back
        else:
            acts[:, pl.ds(0, 2 * HID)] += part
            acts[:, pl.ds(2 * HID, HID)] += back

    forward(c, True)
    forward(2 + c, False)
    def from_other_core(side, pair, j):
        dx = ((0, 1 + 2 * xl), (2, 3 - 2 * xl))[side][pair]
        quarter = 2 * (xh, 1 - xh)[side] + 1 - c
        row = ys[j] * 2 + (xl, 1 - xl)[pair]
        for h in range(2):
            ref = arrays[h][0].at[quarter, row]
            n = dx * 4 + j if h == 0 else j * 4 + dx
            opposite_x, same_x = side == 1 and pair == 0, side == 0 and pair == 0
            second_half = None
            if h == 0:
                second_half = 16 + dx if j == 2 else 20 if opposite_x and j == 0 else None
            else:
                second_half = 16 + j if opposite_x else 20 if same_x and j == 2 else None
            pieces = [(n, ref)]
            if second_half is not None:
                pieces = [(n, ref.at[:, pl.ds(0, HALF)]), (second_half, ref.at[:, pl.ds(HALF, HALF)])]
            for m, part in pieces:
                remote(part, part, ds_sem.at[h, m], dr_sem.at[h, m], sibling).wait_recv()

    for side in range(2):
        for pair in range(2):
            for j in range(4):
                from_other_core(side, pair, j)
        forward(2 * (xh, 1 - xh)[side] + 1 - c, False)
    gate, up, dh = acts[:, pl.ds(0, HID)], acts[:, pl.ds(HID, HID)], acts[:, pl.ds(2 * HID, HID)]
    sigma = jax.nn.sigmoid(gate)
    active = gate * sigma
    hid[...] = (active * up).astype(BF)
    dcat[:, pl.ds(0, HID)] = (dh * up * (sigma + active * (1.0 - sigma))).astype(BF)
    dcat[:, pl.ds(HID, HID)] = (dh * active).astype(BF)

    sides = ((sl1, rl1, sl2, rl2), (sr1, rr1, sr2, rr2))

    def home(h, first, second):
        px, py = off(h, first, second)
        return xhs[px], planes[px][py][0]

    def both_cores(h, first, second):
        a, b = home(h, first, second)
        cols = pl.ds(h * HALF, HALF)
        return acc[a, b, :, cols] + rbuf[a, b, :, cols].astype(F32)

    def first_axis(h, d, second):
        s1, r1, _, _ = sides[h]
        s1[d, second] = both_cores(h, d, second).astype(BF)
        sem = ps_sem.at[h, d, second], pr_sem.at[h, d, second]
        send(s1.at[d, second], r1.at[d, second], *sem, at(*off(h, d, 0)))

    near, far = xh, 1 - xh

    def piece(ref, i, h):
        return ref.at[(far, near)[i], :, :, pl.ds(h * HALF, HALF)]

    for i, a in enumerate((far, near)):
        for h in (1, 0):
            cols = pl.ds(h * HALF, HALF)
            sbuf[a, :, :, cols] = dot(dcat[...], wgut[2 * a + 1 - c, :, cols]).astype(BF).reshape(NG, GROUP, HALF)
            send(piece(sbuf, i, h), piece(rbuf, i, h), es_sem.at[i, h], er_sem.at[i, h], sibling)

    def from_sibling(i, h):
        remote(piece(sbuf, i, h), piece(rbuf, i, h), es_sem.at[i, h], er_sem.at[i, h], sibling).wait_recv()

    acc[far] = dot(dcat[...], wgut[2 * far + c]).reshape(NG, GROUP, QF)
    from_sibling(0, 1)
    for d in (2, 1, 3):
        first_axis(1, d, 2)
    from_sibling(0, 0)
    for second in (2, 1, 3, 0):
        first_axis(0, 2, second)
    acc[near] = dot(dcat[...], wgut[2 * near + c]).reshape(NG, GROUP, QF)
    for h in (1, 0):
        from_sibling(1, h)
    for second in (2, 1, 3, 0):
        for d in (1, 3):
            first_axis(0, d, second)
        if second != 2:
            for d in (2, 1, 3):
                first_axis(1, d, second)

    for second in (2, 1, 3, 0):
        for h in range(2):
            s1, r1, s2, r2 = sides[h]
            total = both_cores(h, 0, second)
            for d in range(1, 4):
                sem = ps_sem.at[h, d, second], pr_sem.at[h, d, second]
                remote(s1.at[d, second], r1.at[d, second], *sem, sibling).wait_recv()
                total = total + r1[d, second].astype(F32)
            if second == 0:
                mine[:, pl.ds(h * HALF, HALF)] = total
            else:
                s2[second] = total.astype(BF)
                send(s2.at[second], r2.at[second], qs_sem.at[h, second], qr_sem.at[h, second], at(*off(h, 0, second)))
    for h in range(2):
        s1, r1, s2, r2 = sides[h]
        total = mine[:, pl.ds(h * HALF, HALF)]
        for d in range(1, 4):
            remote(s2.at[d], r2.at[d], qs_sem.at[h, d], qr_sem.at[h, d], sibling).wait_recv()
            total = total + r2[d].astype(F32)
        zsum[:, pl.ds(h * HALF, HALF)] = total.astype(BF)

    r = lax.broadcasted_iota(jnp.int32, (NZ * 16, GROUP), 0)
    s = lax.broadcasted_iota(jnp.int32, (NZ * 16, GROUP), 1)
    packed = jnp.zeros((NZ * 16, 256), F32)
    for third in range(3):
        k = r % 16 - 3 * third
        place = ((k >= 0) & (k < TOK) & (s == (r // 16) * TOK + k)).astype(F32).astype(BF)
        packed = packed + dot(place, zsum[:, pl.ds(256 * third, 256)])
    sz[...] = packed.astype(BF).reshape(NZ, 16, 256)
    def hand_in(step, d):
        send(sz.at[zs[d % NZ]], rz.at[-d % NZ], fs_sem.at[-d % NZ], fr_sem.at[-d % NZ], zdev(step))

    def handed(d):
        remote(sz.at[z], rz.at[d % NZ], fs_sem.at[d % NZ], fr_sem.at[d % NZ], sibling).wait_recv()
        return rz[d % NZ].astype(F32)

    for away in (8, 7, 6, 5):
        hand_in(4 - away, -away)
    for away in (7, 6, 5):
        hand_in(away - 4, away)
    for d in (3, -3, 2, -2, 1, -1):
        hand_in(d, d)
    for q in range(NQ):
        both = lax.dot_general(
            tk[q].reshape(ROWS, QF), dcat[...], (((0,), (0,)), ((), ())), preferred_element_type=F32
        ).astype(BF)
        gg_ref[0, pl.ds(q * QF, QF), :] = both[:, :HID]
        gu_ref[0, pl.ds(q * QF, QF), :] = both[:, HID:]

    for hub, fars in ((4, (5, 6, 7, 8)), (-4, (-5, -6, -7))):
        ref = sz.at[zs[-hub % NZ]]
        total = ref[...].astype(F32)
        for far in fars:
            total = total + handed(far)
        ref[...] = total.astype(BF)
        hand_in(-hub, -hub)
    hid_t = hid[...].T
    for q in range(NQ):
        gd_ref[0, :, pl.ds(q * QF, QF)] = dot(hid_t, g[q]).astype(BF)

    total = sz[z].astype(F32)
    for d in (1, -1, 2, -2, 3, -3, 4, -4):
        total = total + handed(d)
    stage[:, pl.ds(0, 256)] = total
    for third in range(3):
        gx_ref[:, pl.ds(256 * third, 256)] = stage[pl.ds(3 * third, TOK), pl.ds(0, 256)].astype(BF)

    for copy in sends:
        copy.wait_send()


def settle(*refs):
    copies = [pltpu.make_async_copy(refs[i], refs[4 + i], refs[8].at[i]) for i in range(4)]
    for copy in copies:
        copy.start()
    for copy in copies:
        copy.wait()


def shards(tokens, out_grad, expert_ids, gate_weights, w_gate, w_up, w_down):
    vmem = pl.BlockSpec(memory_space=pltpu.VMEM)
    anywhere = pl.BlockSpec(memory_space=pl.ANY)
    dma = pltpu.SemaphoreType.DMA
    results = pl.pallas_call(
        kernel,
        out_shape=(
            pltpu.VMEM((TOK, QF), BF),
            pltpu.VMEM((1, D, HID), BF),
            pltpu.VMEM((1, D, HID), BF),
            pltpu.VMEM((1, HID, D), BF),
        ),
        in_specs=[anywhere] * 7,
        out_specs=(vmem,) * 4,
        scratch_shapes=[
            pltpu.VMEM((TOK, QF), BF),
            pltpu.VMEM((TOK, QF), BF),
            pltpu.SMEM((2, TOK), jnp.int32),
            pltpu.SMEM((2, TOK), F32),
            pltpu.VMEM((16, HALF), F32),
            pltpu.VMEM((NZ, 16, HALF), BF),
            pltpu.VMEM((NQ, NG, GROUP, QF), BF),
            pltpu.VMEM((NQ, NG, GROUP, QF), BF),
            pltpu.VMEM((NG, GROUP, 128), BF),
            pltpu.VMEM((NQ, ROWS, QF), BF),
            pltpu.VMEM((NQ, QF, 2 * HID), BF),
            pltpu.VMEM((NQ, 2 * HID, QF), BF),
            pltpu.VMEM((HID, D), BF),
            pltpu.VMEM((NQ, QF, HID), BF),
            pltpu.VMEM((ROWS, 3 * HID), F32),
            pltpu.VMEM((ROWS, 2 * HID), BF),
            pltpu.VMEM((ROWS, HID), BF),
            pltpu.VMEM((2, NG, GROUP, QF), F32),
            pltpu.VMEM((2, NG, GROUP, QF), BF),
            pltpu.VMEM((2, NG, GROUP, QF), BF),
            pltpu.VMEM((4, 4, GROUP, HALF), BF),
            pltpu.VMEM((4, 4, GROUP, HALF), BF),
            pltpu.VMEM((4, 4, GROUP, HALF), BF),
            pltpu.VMEM((4, 4, GROUP, HALF), BF),
            pltpu.VMEM((4, GROUP, HALF), BF),
            pltpu.VMEM((4, GROUP, HALF), BF),
            pltpu.VMEM((4, GROUP, HALF), BF),
            pltpu.VMEM((4, GROUP, HALF), BF),
            pltpu.VMEM((NZ, 16, 256), BF),
            pltpu.VMEM((NZ, 16, 256), BF),
            pltpu.VMEM((GROUP, QF), BF),
            pltpu.VMEM((GROUP, QF), F32),
            dma((4,)),
            dma((2 * NQ + 1,)),
            dma((NZ,)), dma((NZ,)),
            dma((7,)), dma((7,)),
            dma((2, 5, 4)), dma((2, 5, 4)),
            dma((2, 21)), dma((2, 21)),
            dma((2, 2)), dma((2, 2)),
            dma((2, 4, 4)), dma((2, 4, 4)),
            dma((2, 4)), dma((2, 4)),
            dma((NZ,)), dma((NZ,)),
        ],
        compiler_params=pltpu.CompilerParams(
            collective_id=0, has_side_effects=True, vmem_limit_bytes=56 * 2**20
        ),
        cost_estimate=pl.CostEstimate(flops=2_400_000_000, bytes_accessed=4_800_000, transcendentals=49152),
        name="moe_backward",
    )(tokens, out_grad, expert_ids.T, gate_weights.T, w_gate, w_up, w_down)
    return pl.pallas_call(
        settle,
        out_shape=[jax.ShapeDtypeStruct(v.shape, v.dtype) for v in results],
        in_specs=[anywhere] * 4,
        out_specs=[anywhere] * 4,
        scratch_shapes=[dma((4,))],
        compiler_params=pltpu.CompilerParams(vmem_limit_bytes=2**20),
        name="settle",
    )(*results)


def solution(mesh):
    placed = (
        P("dp", "expert"),
        P("dp", "expert"),
        P("dp", None),
        P("dp", None),
        P("expert", None, "dp"),
        P("expert", None, "dp"),
        P("expert", "dp", None),
    )
    return jax.shard_map(
        shards,
        mesh=mesh,
        in_specs=placed,
        out_specs=(
            P("dp", "expert"),
            P("expert", None, "dp"),
            P("expert", None, "dp"),
            P("expert", "dp", None),
        ),
        check_vma=False,
    )
```
